32 devices in a mesh: dp: 8 (over y, x, core), tensor: 4 (over z).
Axes of the slice: x: 2, y: 2, z: 4, core: 2. Of those that a mesh axis runs over, the one named last changes fastest.
Arguments:
- tokens: bfloat16 [4736, 6144], P(('dp', 'tensor')), parts along dimension 0, may hold values from -3 to 3
- query_weight: bfloat16 [6144, 3072], P(None, 'tensor'), may hold values from -0.078125 to 0.078125
- key_weight: bfloat16 [6144, 3072], P(None, 'tensor'), may hold values from -0.078125 to 0.078125
- value_weight: bfloat16 [6144, 3072], P(None, 'tensor'), may hold values from -0.078125 to 0.078125
- adapter_down_weight: bfloat16 [6144, 32], replicated, may hold values from -0.078125 to 0.078125
- query_adapter_up_weight: bfloat16 [16, 3072], P(None, 'tensor'), may hold values from -0.59765625 to 0.59765625
- value_adapter_up_weight: bfloat16 [16, 3072], P(None, 'tensor'), may hold values from -0.59765625 to 0.59765625
- query_norm_gain: float32 [3072], P('tensor'), may hold values from 1 to 2
- key_norm_gain: float32 [3072], P('tensor'), may hold values from 1 to 2
- output_weight: bfloat16 [3072, 6144], P('tensor'), may hold values from -0.109375 to 0.109375
- reassemble_weight: bfloat16 [6144, 512], P('tensor'), may hold values from -0.078125 to 0.078125
- joining_kernel: bfloat16 [3, 3, 512, 256], replicated, may hold values from -0.09375 to 0.09375
- opening_residual_kernel: bfloat16 [3, 3, 256, 256], replicated, may hold values from -0.125 to 0.125
- closing_residual_kernel: bfloat16 [3, 3, 256, 256], replicated, may hold values from -0.125 to 0.125
Outputs:
- layer_out: bfloat16 [4736, 6144], P(('dp', 'tensor')), parts along dimension 0
- joined_map: bfloat16 [64, 74, 256], P(('dp', 'tensor')), parts along dimension 0
The draws below stay inside these ranges and needn't reach their ends.
There are 8 independent parts, one for each index of `dp`. The reference program is written for one: setup_inputs(seed, part) draws one part's arguments, and reference() takes and returns one part's arrays. A program takes and returns all parts, laid end to end along the dimension named above; an argument that names none is the same for every part. Nothing has to cross between parts.
All inputs are finite; a program needn't handle non-finite values.
Results may differ from the reference program's by a relative error of at most 0.018.
Values may be sent and summed in bfloat16 or wider, within the bound.
No kernel may reach another device: no remote copies, remote signals or barrier semaphores. Data moves between devices by JAX's collectives and lax.ppermute only.
A program may use at most 192 MiB of HBM per device.

```python
import math
import jax
import jax.numpy as jnp
from jax import lax

MODEL_DIMENSION = 6144
HEADS = 24
HEAD_DIM = 128
ADAPTER_RANK = 16
MAP_W = 74
REASM = 512
FEAT = 256
HEADS_WIDTH = 3072
MAP_ROWS = 8
TOKENS = 592
N_TENSOR = 4


def shard_levels(stream_key, extent, cuts, low, high):
    def one(position, blocks):
        steps = jax.random.uniform(jax.random.fold_in(jax.random.fold_in(stream_key, 6), position), (blocks,), jnp.float32, low / len(cuts), high / len(cuts))
        return jnp.repeat(jnp.exp(steps), extent[position] // blocks).reshape((-1,) + (1,) * (len(extent) - position - 1))

    gain = one(*cuts[0])
    for cut in cuts[1:]:
        gain = gain * one(*cut)
    return gain


def centred(rng, dims, scale, most, cuts=(), kind=jnp.bfloat16):
    drawn = jax.random.normal(rng, dims, jnp.float32) * scale
    if len(cuts) > 0:
        drawn = shard_levels(rng, dims, cuts, -0.22, 0.18) * drawn
    return jnp.clip(drawn, min=-most, max=most).astype(kind)


def setup_inputs(seed: int = 0, part: int = 0) -> dict:
    seeds = jax.random.split(jax.random.key(seed), 15)
    own_keys = jax.random.split(jax.random.fold_in(seeds[14], part), 15)
    return {
        "tokens": centred(own_keys[0], (TOKENS, MODEL_DIMENSION), 0.5, 3.0, ((0, 4),)),
        "query_weight": centred(seeds[1], (MODEL_DIMENSION, HEADS_WIDTH), MODEL_DIMENSION ** -0.5, 0.078125, ((1, 4),)),
        "key_weight": centred(seeds[2], (MODEL_DIMENSION, HEADS_WIDTH), MODEL_DIMENSION ** -0.5, 0.078125, ((1, 4),)),
        "value_weight": centred(seeds[3], (MODEL_DIMENSION, HEADS_WIDTH), MODEL_DIMENSION ** -0.5, 0.078125, ((1, 4),)),
        "adapter_down_weight": centred(seeds[4], (MODEL_DIMENSION, 2 * ADAPTER_RANK), MODEL_DIMENSION ** -0.5, 0.078125),
        "query_adapter_up_weight": centred(seeds[5], (ADAPTER_RANK, HEADS_WIDTH), 0.1, 0.59765625, ((1, 4),)),
        "value_adapter_up_weight": centred(seeds[6], (ADAPTER_RANK, HEADS_WIDTH), 0.1, 0.59765625, ((1, 4),)),
        "query_norm_gain": jnp.clip(jnp.exp(math.log(2.0) - 0.6931472 * jax.random.uniform(seeds[7], (HEADS_WIDTH,), jnp.float32) ** shard_levels(seeds[7], (HEADS_WIDTH,), ((0, 4),), -0.2, 0.2)), 1.0, 2.0),
        "key_norm_gain": jnp.clip(jnp.exp(math.log(2.0) - 0.6931472 * jax.random.uniform(seeds[8], (HEADS_WIDTH,), jnp.float32) ** shard_levels(seeds[8], (HEADS_WIDTH,), ((0, 4),), -0.2, 0.2)), 1.0, 2.0),
        "output_weight": centred(seeds[9], (HEADS_WIDTH, MODEL_DIMENSION), HEADS_WIDTH ** -0.5, 0.109375, ((0, 4),)),
        "reassemble_weight": centred(seeds[10], (MODEL_DIMENSION, REASM), MODEL_DIMENSION ** -0.5, 0.078125, ((0, 4),)),
        "joining_kernel": centred(seeds[11], (3, 3, REASM, FEAT), (9 * REASM) ** -0.5, 0.09375),
        "opening_residual_kernel": centred(seeds[12], (3, 3, FEAT, FEAT), (9 * FEAT) ** -0.5, 0.125),
        "closing_residual_kernel": centred(seeds[13], (3, 3, FEAT, FEAT), (9 * FEAT) ** -0.5, 0.125),
    }


epsilon = 1e-06
adapter_scale = 2.0

def normalize(values):
    average = lax.optimization_barrier(jnp.mean(values, axis=-1, keepdims=True))
    centered = values - average
    variance = lax.optimization_barrier(jnp.mean(centered * centered, axis=-1, keepdims=True))
    return centered * lax.rsqrt(variance + epsilon)

def conv_same(field, kernel):
    padded = jnp.pad(field, ((1, 1), (1, 1), (0, 0)))
    row_count = field.shape[0]
    col_count = field.shape[1]
    running = jnp.zeros((row_count, col_count, kernel.shape[3]), jnp.float32)
    for offset_row in range(3):
        for offset_col in range(3):
            window = padded[offset_row:offset_row + row_count, offset_col:offset_col + col_count, :]
            running = running + jnp.einsum('rwc,cf->rwf', window.astype(jnp.float32), kernel[offset_row, offset_col].astype(jnp.float32))
    return running

def reference(tokens, query_weight, key_weight, value_weight, adapter_down_weight, query_adapter_up_weight, value_adapter_up_weight, query_norm_gain, key_norm_gain, output_weight, reassemble_weight, joining_kernel, opening_residual_kernel, closing_residual_kernel):
    normalized_input = normalize(tokens.astype(jnp.float32)).astype(jnp.bfloat16)
    reduced_output = jnp.dot(normalized_input, adapter_down_weight, preferred_element_type=jnp.float32).astype(jnp.bfloat16)
    query_matrix = jnp.dot(normalized_input, query_weight, preferred_element_type=jnp.float32) + adapter_scale * jnp.dot(reduced_output[:, :ADAPTER_RANK], query_adapter_up_weight, preferred_element_type=jnp.float32)
    key_rows = jnp.dot(normalized_input, key_weight, preferred_element_type=jnp.float32)
    value_matrix = (jnp.dot(normalized_input, value_weight, preferred_element_type=jnp.float32) + adapter_scale * jnp.dot(reduced_output[:, ADAPTER_RANK:], value_adapter_up_weight, preferred_element_type=jnp.float32)).astype(jnp.bfloat16)
    shape_heads = (TOKENS, HEADS, HEAD_DIM)
    query_heads = (normalize(query_matrix.reshape(shape_heads)) * (query_norm_gain.reshape(HEADS, HEAD_DIM) / math.sqrt(HEAD_DIM))).astype(jnp.bfloat16)
    key_heads = (normalize(key_rows.reshape(shape_heads)) * key_norm_gain.reshape(HEADS, HEAD_DIM)).astype(jnp.bfloat16)
    value_heads = value_matrix.reshape(shape_heads)

    def one_head(operands):
        head_query, head_key, head_value = operands
        scores = jnp.dot(head_query, head_key.T, preferred_element_type=jnp.float32)
        raised = jnp.exp(scores)
        softmax_weights = (raised / lax.optimization_barrier(jnp.sum(raised, axis=-1, keepdims=True))).astype(jnp.bfloat16)
        return jnp.dot(softmax_weights, head_value, preferred_element_type=jnp.float32).astype(jnp.bfloat16)
    per_head = lax.map(one_head, (jnp.transpose(query_heads, (1, 0, 2)), jnp.transpose(key_heads, (1, 0, 2)), jnp.transpose(value_heads, (1, 0, 2))))
    attended = jnp.transpose(per_head, (1, 0, 2)).reshape(TOKENS, HEADS * HEAD_DIM)
    group_width = HEADS * HEAD_DIM // N_TENSOR
    head_sum = jnp.zeros((TOKENS, MODEL_DIMENSION), jnp.float32)
    for head_group in range(N_TENSOR):
        lower = head_group * group_width
        partial_sum = jnp.dot(attended[:, lower:lower + group_width], output_weight[lower:lower + group_width], preferred_element_type=jnp.float32)
        rounded = lax.optimization_barrier(partial_sum.astype(jnp.bfloat16))
        head_sum = head_sum + rounded.astype(jnp.float32)
    layer_out = (tokens.astype(jnp.float32) + head_sum).astype(jnp.bfloat16)
    reassembled = jnp.dot(layer_out, reassemble_weight, preferred_element_type=jnp.float32).astype(jnp.bfloat16).reshape(MAP_ROWS, MAP_W, REASM)
    feature = conv_same(reassembled, joining_kernel).astype(jnp.bfloat16)
    inner_field = jax.nn.relu(conv_same(jax.nn.relu(feature), opening_residual_kernel)).astype(jnp.bfloat16)
    joined_map = (conv_same(inner_field, closing_residual_kernel) + feature.astype(jnp.float32)).astype(jnp.bfloat16)
    return (layer_out, joined_map)
```

```python
import math

import jax
import jax.numpy as jnp
from jax import lax
from jax.sharding import PartitionSpec as P

HEAD_DIM = 128
MAP_W = 74


epsilon = 1e-06
adapter_scale = 2.0


def padded_2(value, sides, width):
    for axis, dim in sides:
        count, length = (lax.axis_size(axis), value.shape[dim])
        up = [(i, (i + 1) % count) for i in range(count - 1)]
        down = [(j, i) for i, j in up]
        last = lax.slice_in_dim(value, length - width, length, axis=dim)
        initial = lax.slice_in_dim(value, 0, width, axis=dim)
        before = lax.ppermute(last, axis, up)
        after = lax.ppermute(initial, axis, down)
        value = jnp.concatenate([before, value, after], axis=dim)
    return value


def normalize(values):
    average = jnp.mean(values, axis=-1, keepdims=True)
    centered = values - average
    variance = jnp.mean(centered * centered, axis=-1, keepdims=True)
    return centered * lax.rsqrt(variance + epsilon)


def conv_valid(padded, kernel):
    row_count = padded.shape[0] - 2
    col_count = padded.shape[1] - 2
    running = jnp.zeros((row_count, col_count, kernel.shape[3]), jnp.float32)
    for offset_row in range(3):
        for offset_col in range(3):
            window = padded[
                offset_row : offset_row + row_count, offset_col : offset_col + col_count, :
            ]
            running = running + jnp.einsum(
                "rwc,cf->rwf",
                window,
                kernel[offset_row, offset_col],
                preferred_element_type=jnp.float32,
            )
    return running


def pad_columns(field):
    return jnp.pad(field, ((0, 0), (1, 1), (0, 0)))


def extend_rows(field):
    return padded_2(field, (("tensor", 0),), 1)


def attend(
    normalized_input,
    query_weight,
    key_weight,
    value_weight,
    adapter_down_weight,
    query_adapter_up_weight,
    value_adapter_up_weight,
    query_norm_gain,
    key_norm_gain,
):
    reduced_rows = query_adapter_up_weight.shape[0]
    reduced_output = jnp.dot(
        normalized_input, adapter_down_weight, preferred_element_type=jnp.float32
    ).astype(jnp.bfloat16)
    query_matrix = jnp.dot(
        normalized_input, query_weight, preferred_element_type=jnp.float32
    ) + adapter_scale * jnp.dot(
        reduced_output[:, :reduced_rows],
        query_adapter_up_weight,
        preferred_element_type=jnp.float32,
    )
    key_rows = jnp.dot(normalized_input, key_weight, preferred_element_type=jnp.float32)
    value_matrix = (
        jnp.dot(normalized_input, value_weight, preferred_element_type=jnp.float32)
        + adapter_scale
        * jnp.dot(
            reduced_output[:, reduced_rows:],
            value_adapter_up_weight,
            preferred_element_type=jnp.float32,
        )
    ).astype(jnp.bfloat16)
    token_count = normalized_input.shape[0]
    head_count = query_weight.shape[1] // HEAD_DIM
    shape_heads = (token_count, head_count, HEAD_DIM)
    query_heads = (
        normalize(query_matrix.reshape(shape_heads))
        * (query_norm_gain.reshape(head_count, HEAD_DIM) / math.sqrt(HEAD_DIM))
    ).astype(jnp.bfloat16)
    key_heads = (
        normalize(key_rows.reshape(shape_heads)) * key_norm_gain.reshape(head_count, HEAD_DIM)
    ).astype(jnp.bfloat16)
    scores = jnp.einsum("qhd,khd->hqk", query_heads, key_heads, preferred_element_type=jnp.float32)
    raised = jnp.exp(scores)
    softmax_weights = (raised / jnp.sum(raised, axis=-1, keepdims=True)).astype(jnp.bfloat16)
    attended = jnp.einsum(
        "hqk,khd->qhd",
        softmax_weights,
        value_matrix.reshape(shape_heads),
        preferred_element_type=jnp.float32,
    )
    return attended.astype(jnp.bfloat16).reshape(token_count, head_count * HEAD_DIM)


def on_device(
    tokens,
    query_weight,
    key_weight,
    value_weight,
    adapter_down_weight,
    query_adapter_up_weight,
    value_adapter_up_weight,
    query_norm_gain,
    key_norm_gain,
    output_weight,
    reassemble_weight,
    joining_kernel,
    opening_residual_kernel,
    closing_residual_kernel,
):
    local_rows = tokens.shape[0]
    model_width = tokens.shape[1]
    everyone = lax.all_gather(tokens, "tensor", axis=0, tiled=True)
    normalized_input = normalize(everyone.astype(jnp.float32)).astype(jnp.bfloat16)
    attended = attend(
        normalized_input,
        query_weight,
        key_weight,
        value_weight,
        adapter_down_weight,
        query_adapter_up_weight,
        value_adapter_up_weight,
        query_norm_gain,
        key_norm_gain,
    )
    partials = jnp.dot(attended, output_weight, preferred_element_type=jnp.float32)
    column_sum = lax.psum_scatter(
        partials.astype(jnp.bfloat16), "tensor", scatter_dimension=1, tiled=True
    ).astype(jnp.float32)
    slice_width = model_width // lax.axis_size("tensor")
    own_columns = lax.dynamic_slice_in_dim(
        everyone, lax.axis_index("tensor") * slice_width, slice_width, 1
    )
    layer_columns = (own_columns.astype(jnp.float32) + column_sum).astype(jnp.bfloat16)
    layer_out = lax.all_to_all(layer_columns, "tensor", split_axis=0, concat_axis=1, tiled=True)
    reassembled = lax.psum_scatter(
        jnp.dot(layer_columns, reassemble_weight, preferred_element_type=jnp.float32).astype(
            jnp.bfloat16
        ),
        "tensor",
        scatter_dimension=0,
        tiled=True,
    )
    map_strip = reassembled.reshape(local_rows // MAP_W, MAP_W, reassemble_weight.shape[1])
    rimmed = padded_2(map_strip, (("tensor", 0),), 1)
    feature = conv_valid(pad_columns(rimmed), joining_kernel).astype(jnp.bfloat16)
    inner_field = jax.nn.relu(
        conv_valid(pad_columns(extend_rows(jax.nn.relu(feature))), opening_residual_kernel)
    ).astype(jnp.bfloat16)
    joined_map = (
        conv_valid(pad_columns(extend_rows(inner_field)), closing_residual_kernel)
        + feature.astype(jnp.float32)
    ).astype(jnp.bfloat16)
    return (layer_out, joined_map)


CHUNKS = 3


def project(parts, weights, adapters):
    query_weight, key_weight, value_weight, adapter_down_weight = weights
    query_up, value_up = adapters
    width = parts[0].shape[1]
    rank = query_up.shape[0]

    def dot(weight):
        total = None
        for i, part in enumerate(parts):
            term = jnp.dot(
                part,
                weight[i * width : (i + 1) * width],
                preferred_element_type=jnp.float32,
            )
            total = term if total is None else total + term
        return total

    low = dot(adapter_down_weight).astype(jnp.bfloat16)
    query = dot(query_weight) + adapter_scale * jnp.dot(
        low[:, :rank], query_up, preferred_element_type=jnp.float32
    )
    key = dot(key_weight)
    value = dot(value_weight) + adapter_scale * jnp.dot(
        low[:, rank:], value_up, preferred_element_type=jnp.float32
    )
    return query, key, value.astype(jnp.bfloat16)


def heads_attention(query_matrix, key_rows, value_matrix, query_norm_gain, key_norm_gain):
    token_count = query_matrix.shape[0]
    head_count = query_matrix.shape[1] // HEAD_DIM
    shape_heads = (token_count, head_count, HEAD_DIM)
    query_heads = (
        normalize(query_matrix.reshape(shape_heads))
        * (query_norm_gain.reshape(head_count, HEAD_DIM) / math.sqrt(HEAD_DIM))
    ).astype(jnp.bfloat16)
    key_heads = (
        normalize(key_rows.reshape(shape_heads)) * key_norm_gain.reshape(head_count, HEAD_DIM)
    ).astype(jnp.bfloat16)
    scores = jnp.einsum("qhd,khd->hqk", query_heads, key_heads, preferred_element_type=jnp.float32)
    raised = jnp.exp(scores)
    softmax_weights = (raised / jnp.sum(raised, axis=-1, keepdims=True)).astype(jnp.bfloat16)
    attended = jnp.einsum(
        "hqk,khd->qhd",
        softmax_weights,
        value_matrix.reshape(shape_heads),
        preferred_element_type=jnp.float32,
    )
    return attended.astype(jnp.bfloat16).reshape(token_count, head_count * HEAD_DIM)


def joining(reassembled, joining_kernel, opening_residual_kernel, closing_residual_kernel):
    count = lax.axis_size("tensor")
    place = lax.axis_index("tensor")
    rows = reassembled.shape[0]
    send = lambda value, step: lax.ppermute(
        value,
        "tensor",
        [(i, i + step) for i in range(count) if 0 <= i + step < count],
    )
    above = send(reassembled, 1)
    below = send(reassembled, -1)
    above_far = send(reassembled[rows - 1 :], 2)
    below_far = send(reassembled[:1], -2)
    extended = jnp.concatenate([above_far, above, reassembled, below, below_far], axis=0)
    first = place * rows
    total = count * rows

    def inside(field, margin):
        index = first - margin + jnp.arange(field.shape[0])
        return jnp.where(((index >= 0) & (index < total))[:, None, None], field, 0)

    feature = inside(conv_valid(pad_columns(extended), joining_kernel).astype(jnp.bfloat16), 2)
    inner = inside(
        jax.nn.relu(
            conv_valid(pad_columns(jax.nn.relu(feature)), opening_residual_kernel)
        ).astype(jnp.bfloat16),
        1,
    )
    return (
        conv_valid(pad_columns(inner), closing_residual_kernel)
        + feature[2 : 2 + rows].astype(jnp.float32)
    ).astype(jnp.bfloat16)


def on_device_line(
    tokens,
    query_weight,
    key_weight,
    value_weight,
    adapter_down_weight,
    query_adapter_up_weight,
    value_adapter_up_weight,
    query_norm_gain,
    key_norm_gain,
    output_weight,
    reassemble_weight,
    joining_kernel,
    opening_residual_kernel,
    closing_residual_kernel,
):
    place = lax.axis_index("tensor")
    images = lax.axis_size("dp")
    image = lax.axis_index("dp")
    rows, model_width = tokens.shape
    send = lambda value, pairs: lax.ppermute(value, "tensor", pairs)
    bf16 = jnp.bfloat16

    normed = normalize(tokens.astype(jnp.float32)).astype(bf16)
    width = model_width // CHUNKS
    own = [normed[:, i * width : (i + 1) * width] for i in range(CHUNKS)]

    up1 = [send(part, [(0, 1), (1, 2), (2, 3)]) for part in own]
    down1 = [send(part, [(1, 0), (2, 1), (3, 2)]) for part in own]
    two = []
    last = []
    for i in range(CHUNKS):
        up2 = send(up1[i], [(1, 2), (2, 3)])
        down2 = send(down1[i], [(2, 1), (1, 0)])
        two.append(up2 + down2)
        last.append(send(two[i], [(2, 3), (1, 0)]))

    heads_width = output_weight.shape[0]
    share = heads_width // images
    piece = lax.dynamic_slice_in_dim(output_weight, image * share, share, 0)
    piece, _ = lax.optimization_barrier((piece, (up1[-1], down1[-1])))
    piece = send(piece, [(0, 1), (3, 2)])
    partner_weight = lax.all_gather(piece, "dp", axis=0, tiled=True)

    slice_rows = reassemble_weight.shape[0] // images
    small = lax.dynamic_slice_in_dim(reassemble_weight, image * slice_rows, slice_rows, 0)
    small, _ = lax.optimization_barrier((small, partner_weight))
    small = lax.all_gather(small, "tensor", axis=0, tiled=False)
    reassemble_full = lax.all_gather(small, "dp", axis=1, tiled=True).reshape(
        model_width, reassemble_weight.shape[1]
    )

    weights = (query_weight, key_weight, value_weight, adapter_down_weight)
    adapters = (query_adapter_up_weight, value_adapter_up_weight)
    own_qkv = project(own, weights, adapters)
    one_qkv = project(
        [jnp.concatenate([u, d], axis=0) for u, d in zip(up1, down1)], weights, adapters
    )
    two_qkv = project(two, weights, adapters)
    last_qkv = project(last, weights, adapters)

    def ordered(a, b, c, d):
        previous = jnp.where(place == 0, d, b[:rows])
        following = jnp.where(place == 3, d, b[rows:])
        return jnp.concatenate([a, following, c, previous], axis=0)

    query, key, value = (
        ordered(*parts) for parts in zip(own_qkv, one_qkv, two_qkv, last_qkv)
    )
    attended = heads_attention(query, key, value, query_norm_gain, key_norm_gain)
    attended = attended.reshape(4, rows, heads_width)
    pick = lambda index: lax.dynamic_index_in_dim(attended, index, 0, keepdims=False)

    outward = [(0, 1), (3, 2)]
    got_far = send(pick(jnp.where(place == 0, 3, 1)), outward)
    got_near = send(attended[2], outward)
    got_own = send(pick(jnp.where(place == 0, 1, 3)), outward)

    dot = lambda a, b: jnp.dot(a, b, preferred_element_type=jnp.float32)
    edge = dot(pick(jnp.where(place == 1, 3, 1)), output_weight).astype(bf16)
    edge = send(edge, [(1, 0), (2, 3)])
    far = (dot(attended[2], output_weight) + dot(got_far, partner_weight)).astype(bf16)
    far = send(far, [(1, 3), (2, 0)])
    near = (
        dot(pick(jnp.where(place == 1, 1, 3)), output_weight) + dot(got_near, partner_weight)
    ).astype(bf16)
    near = send(near, [(1, 2), (2, 1)])
    mine = (
        tokens.astype(jnp.float32)
        + dot(attended[0], output_weight)
        + dot(got_own, partner_weight)
    )
    layer_out = (
        mine
        + edge.astype(jnp.float32)
        + far.astype(jnp.float32)
        + near.astype(jnp.float32)
    ).astype(bf16)

    reassembled = dot(layer_out, reassemble_full).astype(bf16)
    reassembled = reassembled.reshape(rows // MAP_W, MAP_W, reassemble_weight.shape[1])
    joined_map = joining(
        reassembled, joining_kernel, opening_residual_kernel, closing_residual_kernel
    )
    return (layer_out, joined_map)


def solution(mesh):
    body = on_device_line if mesh.shape["tensor"] == 4 else on_device
    return jax.shard_map(
        body,
        mesh=mesh,
        in_specs=(
            P(("dp", "tensor"), None),
            P(None, "tensor"),
            P(None, "tensor"),
            P(None, "tensor"),
            P(),
            P(None, "tensor"),
            P(None, "tensor"),
            P("tensor"),
            P("tensor"),
            P("tensor", None),
            P("tensor", None),
            P(),
            P(),
            P(),
        ),
        out_specs=(P(("dp", "tensor"), None), P(("dp", "tensor"), None, None)),
        check_vma=False,
    )
```

```python
import functools
import math

import jax
import jax.numpy as jnp
from jax import lax
from jax.experimental import pallas as pl
from jax.experimental.pallas import tpu as pltpu
from jax.sharding import PartitionSpec as P

HEAD_DIM = 128
MAP_W = 74


epsilon = 1e-06
adapter_scale = 2.0


def padded_2(value, sides, width):
    for axis, dim in sides:
        count, length = (lax.axis_size(axis), value.shape[dim])
        up = [(i, (i + 1) % count) for i in range(count - 1)]
        down = [(j, i) for i, j in up]
        last = lax.slice_in_dim(value, length - width, length, axis=dim)
        initial = lax.slice_in_dim(value, 0, width, axis=dim)
        before = lax.ppermute(last, axis, up)
        after = lax.ppermute(initial, axis, down)
        value = jnp.concatenate([before, value, after], axis=dim)
    return value


def normalize(values):
    average = jnp.mean(values, axis=-1, keepdims=True)
    centered = values - average
    variance = jnp.mean(centered * centered, axis=-1, keepdims=True)
    return centered * lax.rsqrt(variance + epsilon)


def conv_valid(padded, kernel):
    row_count = padded.shape[0] - 2
    col_count = padded.shape[1] - 2
    running = jnp.zeros((row_count, col_count, kernel.shape[3]), jnp.float32)
    for offset_row in range(3):
        for offset_col in range(3):
            window = padded[
                offset_row : offset_row + row_count, offset_col : offset_col + col_count, :
            ]
            running = running + jnp.einsum(
                "rwc,cf->rwf",
                window,
                kernel[offset_row, offset_col],
                preferred_element_type=jnp.float32,
            )
    return running


def pad_columns(field):
    return jnp.pad(field, ((0, 0), (1, 1), (0, 0)))


def extend_rows(field):
    return padded_2(field, (("tensor", 0),), 1)


def attend(
    normalized_input,
    query_weight,
    key_weight,
    value_weight,
    adapter_down_weight,
    query_adapter_up_weight,
    value_adapter_up_weight,
    query_norm_gain,
    key_norm_gain,
):
    reduced_rows = query_adapter_up_weight.shape[0]
    reduced_output = jnp.dot(
        normalized_input, adapter_down_weight, preferred_element_type=jnp.float32
    ).astype(jnp.bfloat16)
    query_matrix = jnp.dot(
        normalized_input, query_weight, preferred_element_type=jnp.float32
    ) + adapter_scale * jnp.dot(
        reduced_output[:, :reduced_rows],
        query_adapter_up_weight,
        preferred_element_type=jnp.float32,
    )
    key_rows = jnp.dot(normalized_input, key_weight, preferred_element_type=jnp.float32)
    value_matrix = (
        jnp.dot(normalized_input, value_weight, preferred_element_type=jnp.float32)
        + adapter_scale
        * jnp.dot(
            reduced_output[:, reduced_rows:],
            value_adapter_up_weight,
            preferred_element_type=jnp.float32,
        )
    ).astype(jnp.bfloat16)
    token_count = normalized_input.shape[0]
    head_count = query_weight.shape[1] // HEAD_DIM
    shape_heads = (token_count, head_count, HEAD_DIM)
    query_heads = (
        normalize(query_matrix.reshape(shape_heads))
        * (query_norm_gain.reshape(head_count, HEAD_DIM) / math.sqrt(HEAD_DIM))
    ).astype(jnp.bfloat16)
    key_heads = (
        normalize(key_rows.reshape(shape_heads)) * key_norm_gain.reshape(head_count, HEAD_DIM)
    ).astype(jnp.bfloat16)
    scores = jnp.einsum("qhd,khd->hqk", query_heads, key_heads, preferred_element_type=jnp.float32)
    raised = jnp.exp(scores)
    softmax_weights = (raised / jnp.sum(raised, axis=-1, keepdims=True)).astype(jnp.bfloat16)
    attended = jnp.einsum(
        "hqk,khd->qhd",
        softmax_weights,
        value_matrix.reshape(shape_heads),
        preferred_element_type=jnp.float32,
    )
    return attended.astype(jnp.bfloat16).reshape(token_count, head_count * HEAD_DIM)


def on_device(
    tokens,
    query_weight,
    key_weight,
    value_weight,
    adapter_down_weight,
    query_adapter_up_weight,
    value_adapter_up_weight,
    query_norm_gain,
    key_norm_gain,
    output_weight,
    reassemble_weight,
    joining_kernel,
    opening_residual_kernel,
    closing_residual_kernel,
):
    local_rows = tokens.shape[0]
    model_width = tokens.shape[1]
    everyone = lax.all_gather(tokens, "tensor", axis=0, tiled=True)
    normalized_input = normalize(everyone.astype(jnp.float32)).astype(jnp.bfloat16)
    attended = attend(
        normalized_input,
        query_weight,
        key_weight,
        value_weight,
        adapter_down_weight,
        query_adapter_up_weight,
        value_adapter_up_weight,
        query_norm_gain,
        key_norm_gain,
    )
    partials = jnp.dot(attended, output_weight, preferred_element_type=jnp.float32)
    column_sum = lax.psum_scatter(
        partials.astype(jnp.bfloat16), "tensor", scatter_dimension=1, tiled=True
    ).astype(jnp.float32)
    slice_width = model_width // lax.axis_size("tensor")
    own_columns = lax.dynamic_slice_in_dim(
        everyone, lax.axis_index("tensor") * slice_width, slice_width, 1
    )
    layer_columns = (own_columns.astype(jnp.float32) + column_sum).astype(jnp.bfloat16)
    layer_out = lax.all_to_all(layer_columns, "tensor", split_axis=0, concat_axis=1, tiled=True)
    reassembled = lax.psum_scatter(
        jnp.dot(layer_columns, reassemble_weight, preferred_element_type=jnp.float32).astype(
            jnp.bfloat16
        ),
        "tensor",
        scatter_dimension=0,
        tiled=True,
    )
    map_strip = reassembled.reshape(local_rows // MAP_W, MAP_W, reassemble_weight.shape[1])
    rimmed = padded_2(map_strip, (("tensor", 0),), 1)
    feature = conv_valid(pad_columns(rimmed), joining_kernel).astype(jnp.bfloat16)
    inner_field = jax.nn.relu(
        conv_valid(pad_columns(extend_rows(jax.nn.relu(feature))), opening_residual_kernel)
    ).astype(jnp.bfloat16)
    joined_map = (
        conv_valid(pad_columns(extend_rows(inner_field)), closing_residual_kernel)
        + feature.astype(jnp.float32)
    ).astype(jnp.bfloat16)
    return (layer_out, joined_map)


f32 = jnp.float32
bf16 = jnp.bfloat16
KEY_STEPS = 6
FINISH_STEPS = 4
PAIR_STEPS = 4
HEADS_STEP = 2
LAST_STEPS = 2
ROW_BLOCK = 80
VMEM_LIMIT = 56 * 1024 * 1024


def round_up(value, unit):
    return (value + unit - 1) // unit * unit


def dot32(a, b):
    return jnp.dot(a, b, preferred_element_type=f32)


def rows_kernel(tokens, *outs):
    normed = normalize(tokens[...].astype(f32)).astype(bf16)
    begin = 0
    for out in outs:
        out[...] = normed[:, begin : begin + out.shape[1]]
        begin += out.shape[1]


def normalized_rows(tokens, widths):
    rows, model_width = tokens.shape
    block = lambda width: pl.BlockSpec((ROW_BLOCK, width), lambda r: (r, 0))
    return pl.pallas_call(
        rows_kernel,
        grid=(pl.cdiv(rows, ROW_BLOCK),),
        in_specs=[block(model_width)],
        out_specs=[block(width) for width in widths],
        out_shape=[jax.ShapeDtypeStruct((rows, width), bf16) for width in widths],
        compiler_params=pltpu.CompilerParams(vmem_limit_bytes=VMEM_LIMIT),
        name="normalized_rows",
    )(tokens)


def project_kernel(count, given, final, *refs):
    parts = refs[:count]
    weights = refs[count : count + 3]
    down, query_up, value_up, query_gain, key_gain = refs[count + 3 : count + 8]
    refs = refs[count + 8 :]
    earlier, refs = (refs[:2], refs[2:]) if given else (None, refs)
    outs, (totals, low) = refs[:-2], refs[-2:]
    step = pl.program_id(0)

    @pl.when(step == 0)
    def _():
        for i in range(count):
            for j in range(3):
                term = dot32(parts[i][...], weights[j][...])
                totals[i, j] = term + earlier[0][i, j] if given else term
            term = dot32(parts[i][...], down[...])
            low[i] = term + earlier[1][i] if given else term

    @pl.when(step > 0)
    def _():
        for i in range(count):
            for j in range(3):
                totals[i, j] += dot32(parts[i][...], weights[j][...])
            low[i] += dot32(parts[i][...], down[...])

    @pl.when(step == pl.num_programs(0) - 1)
    def _():
        if not final:
            outs[0][...] = totals[...]
            outs[1][...] = low[...]
            return
        for i in range(count):
            reduced = low[i].astype(bf16)
            query = totals[i, 0] + adapter_scale * dot32(reduced, query_up[...])
            value = totals[i, 2] + adapter_scale * dot32(reduced, value_up[...])
            key = totals[i, 1]
            for h in range(query.shape[1] // HEAD_DIM):
                lanes = slice(h * HEAD_DIM, (h + 1) * HEAD_DIM)
                outs[3 * i][:, lanes] = (
                    normalize(query[:, lanes]) * (query_gain[:, lanes] / math.sqrt(HEAD_DIM))
                ).astype(bf16)
                outs[3 * i + 1][:, lanes] = (
                    normalize(key[:, lanes]) * key_gain[:, lanes]
                ).astype(bf16)
            outs[3 * i + 2][...] = value.astype(bf16)


def project(parts, weights, down, ups, gains, first=0, earlier=(), final=True):
    count = len(parts)
    rows, features = parts[0].shape
    model_width, width = weights[0].shape
    depth = model_width // KEY_STEPS
    offset = first // depth
    rank = down.shape[1]
    whole = lambda *shape: pl.BlockSpec(shape, lambda k: (0,) * len(shape))
    sums = [(count, 3, rows, width), (count, rows, rank)]
    results = [((rows, width), bf16)] * (3 * count) if final else [(x, f32) for x in sums]
    result = pl.pallas_call(
        functools.partial(project_kernel, count, len(earlier) > 0, final),
        grid=(features // depth,),
        in_specs=[pl.BlockSpec((rows, depth), lambda k: (0, k))] * count
        + [pl.BlockSpec((depth, width), lambda k: (k + offset, 0))] * 3
        + [pl.BlockSpec((depth, rank), lambda k: (k + offset, 0))]
        + [whole(rank, width)] * 2
        + [whole(1, width)] * 2
        + [whole(*x.shape) for x in earlier],
        out_specs=[whole(*shape) for shape, _ in results],
        out_shape=[jax.ShapeDtypeStruct(*x) for x in results],
        scratch_shapes=[pltpu.VMEM(shape, f32) for shape in sums],
        compiler_params=pltpu.CompilerParams(vmem_limit_bytes=VMEM_LIMIT),
        name="project",
    )(*parts, *weights, down, *ups, *gains, *earlier)
    if not final:
        return result
    return [tuple(result[3 * i : 3 * i + 3]) for i in range(count)]


def attention_kernel(rows, slot, place, *refs):
    blocks = refs[:15]
    outs = refs[15:19]
    query, key, value = refs[19:]
    where = place[0]

    @pl.when(pl.program_id(0) == 0)
    def _():
        for ref in (query, key, value):
            ref[...] = jnp.zeros_like(ref)
        lane = lax.broadcasted_iota(jnp.int32, (rows, HEAD_DIM), 1)
        ones = jnp.where(lane == 0, 1.0, 0.0).astype(bf16)
        for h in range(HEADS_STEP):
            for i in range(4):
                value[h, i * slot : i * slot + rows, HEAD_DIM:] = ones

    for j in range(3):
        own, before, after, two, last = (blocks[3 * i + j] for i in range(5))

        def hold(i, ref):
            for h in range(HEADS_STEP):
                lanes = slice(h * HEAD_DIM, (h + 1) * HEAD_DIM)
                if j < 2:
                    (query, key)[j][h, i * slot : i * slot + rows] = ref[:, lanes]
                else:
                    value[h, i * slot : i * slot + rows, :HEAD_DIM] = ref[:, lanes]

        hold(0, own)
        hold(2, two)
        for i, end, other in ((1, 3, after), (3, 0, before)):
            pl.when(where == end)(functools.partial(hold, i, last))
            pl.when(where != end)(functools.partial(hold, i, other))

    inner = (where == 1) | (where == 2)
    far = jnp.where(inner, 2, jnp.where(where == 0, 3, 1))
    near = jnp.where(inner, jnp.where(where == 1, 1, 3), 2)
    edge = jnp.where((where == 0) | (where == 2), 1, 3)
    for asked, out in zip((far, near, 0, edge), outs):
        asked_rows = pl.ds(pl.multiple_of(asked * slot, slot), slot)
        for h in range(HEADS_STEP):
            scores = lax.dot_general(
                query[h, asked_rows],
                key[h],
                (((1,), (1,)), ((), ())),
                preferred_element_type=f32,
            )
            sums = dot32(jnp.exp(scores).astype(bf16), value[h])
            result = sums[:, :HEAD_DIM] / sums[:, HEAD_DIM : HEAD_DIM + 1]
            lanes = slice(h * HEAD_DIM, (h + 1) * HEAD_DIM)
            out[:, lanes] = result[:rows].astype(bf16)


def attention(place, *qkv):
    rows, width = qkv[0][0].shape
    slot = round_up(rows, 16)
    columns = HEADS_STEP * HEAD_DIM
    block = pl.BlockSpec((rows, columns), lambda h: (0, h))
    return pl.pallas_call(
        functools.partial(attention_kernel, rows, slot),
        grid=(width // columns,),
        in_specs=[pl.BlockSpec(memory_space=pltpu.SMEM)] + [block] * 15,
        out_specs=[block] * 4,
        out_shape=[jax.ShapeDtypeStruct((rows, width), bf16)] * 4,
        scratch_shapes=[
            pltpu.VMEM((HEADS_STEP, 4 * slot, HEAD_DIM), bf16),
            pltpu.VMEM((HEADS_STEP, 4 * slot, HEAD_DIM), bf16),
            pltpu.VMEM((HEADS_STEP, 4 * slot, 2 * HEAD_DIM), bf16),
        ],
        compiler_params=pltpu.CompilerParams(vmem_limit_bytes=16 * 1024 * 1024),
        name="attention",
    )(place.reshape(1), *(x for block_qkv in qkv for x in block_qkv))


def pair_kernel(mine, other, held, got, out):
    out[...] = (dot32(mine[...], held[...]) + dot32(other[...], got[...])).astype(bf16)


def pair_sum(mine, other, held, got):
    rows, width = mine.shape
    model_width = held.shape[1]
    columns = model_width // PAIR_STEPS
    weight = pl.BlockSpec((width, columns), lambda c: (0, c))
    operand = pl.BlockSpec((rows, width), lambda c: (0, 0))
    return pl.pallas_call(
        pair_kernel,
        grid=(PAIR_STEPS,),
        in_specs=[operand, operand, weight, weight],
        out_specs=pl.BlockSpec((rows, columns), lambda c: (0, c)),
        out_shape=jax.ShapeDtypeStruct((rows, model_width), bf16),
        compiler_params=pltpu.CompilerParams(vmem_limit_bytes=VMEM_LIMIT),
        name="pair_sum",
    )(mine, other, held, got)


def finish_kernel(mine, edge, far, near, weight, layer_out, reassembled, total):
    step = pl.program_id(0)
    rows = reassembled.shape[1]
    layer = (
        mine[...] + edge[...].astype(f32) + far[...].astype(f32) + near[...].astype(f32)
    ).astype(bf16)
    layer_out[...] = layer
    term = dot32(layer, weight[...])

    @pl.when(step == 0)
    def _():
        total[...] = term

    @pl.when(step > 0)
    def _():
        total[...] += term

    @pl.when(step == pl.num_programs(0) - 1)
    def _():
        for r in range(reassembled.shape[0]):
            reassembled[r] = total[r * rows : (r + 1) * rows].astype(bf16)


def finish(mine, edge, far, near, weight):
    rows, model_width = mine.shape
    channels = weight.shape[1]
    steps = FINISH_STEPS
    depth = model_width // steps
    block = pl.BlockSpec((rows, depth), lambda k: (0, k))
    shape = (rows // MAP_W, MAP_W, channels)
    return pl.pallas_call(
        finish_kernel,
        grid=(steps,),
        in_specs=[block] * 4 + [pl.BlockSpec((depth, channels), lambda k: (k, 0))],
        out_specs=[block, pl.BlockSpec(shape, lambda k: (0, 0, 0))],
        out_shape=[
            jax.ShapeDtypeStruct((rows, model_width), bf16),
            jax.ShapeDtypeStruct(shape, bf16),
        ],
        scratch_shapes=[pltpu.VMEM((rows, channels), f32)],
        compiler_params=pltpu.CompilerParams(vmem_limit_bytes=VMEM_LIMIT),
        name="finish",
    )(mine, edge, far, near, weight)


def joining_kernel_body(total_rows, pitch, first, *refs):
    pieces = refs[:5]
    joining, opening, closing, out, field, feature, inner = refs[5:]
    field[...] = jnp.zeros_like(field)
    place = 0
    for piece in pieces:
        for r in range(piece.shape[0]):
            field[place * pitch : place * pitch + MAP_W] = piece[r]
            place += 1

    def conv(source, kernel):
        size = source.shape[0] - 2 * pitch
        sums = []
        for b in range(3):
            running = None
            for a in range(3):
                term = dot32(source[a * pitch : a * pitch + size], kernel[a, b])
                running = term if running is None else running + term
            sums.append(running)
        return sums[1] + pltpu.roll(sums[0], 1, 0) + pltpu.roll(sums[2], size - 1, 0)

    def masked(values, margin):
        size, channels = values.shape
        shape = (size // pitch, pitch, channels)
        row = lax.broadcasted_iota(jnp.int32, shape, 0) + (first[0] - margin)
        column = lax.broadcasted_iota(jnp.int32, shape, 1)
        keep = (row >= 0) & (row < total_rows) & (column < MAP_W)
        return jnp.where(keep, values.reshape(shape), 0.0).reshape(size, channels)

    feature[...] = masked(conv(field, joining), 2).astype(bf16)
    rectified = jnp.maximum(feature[...], 0)
    inner[...] = masked(jax.nn.relu(conv(rectified, opening)), 1).astype(bf16)
    rows = out.shape[0]
    result = conv(inner, closing) + feature[2 * pitch : (2 + rows) * pitch].astype(f32)
    for r in range(rows):
        out[r] = result[r * pitch : r * pitch + MAP_W].astype(bf16)


def joining(reassembled, joining_weight, opening_weight, closing_weight):
    count = lax.axis_size("tensor")
    place = lax.axis_index("tensor")
    rows, _, channels = reassembled.shape
    features = joining_weight.shape[3]
    send = lambda value, pairs: lax.ppermute(value, "tensor", pairs)
    above = send(reassembled, [(i, i + 1) for i in range(count - 1)])
    below = send(reassembled, [(i + 1, i) for i in range(count - 1)])
    edge = jnp.where(place < 2, reassembled[rows - 1 :], reassembled[:1])
    edge = send(edge, [(0, 2), (1, 3), (2, 0), (3, 1)])
    above_far = jnp.where(place >= 2, edge, 0)
    below_far = jnp.where(place < 2, edge, 0)
    pitch = round_up(MAP_W + 1, 16)
    first = (place * rows).astype(jnp.int32).reshape(1)
    return pl.pallas_call(
        functools.partial(joining_kernel_body, count * rows, pitch),
        in_specs=[pl.BlockSpec(memory_space=pltpu.SMEM)]
        + [pl.BlockSpec(memory_space=pltpu.VMEM)] * 8,
        out_specs=pl.BlockSpec(memory_space=pltpu.VMEM),
        out_shape=jax.ShapeDtypeStruct((rows, MAP_W, features), bf16),
        scratch_shapes=[
            pltpu.VMEM(((rows + 6) * pitch, channels), bf16),
            pltpu.VMEM(((rows + 4) * pitch, features), bf16),
            pltpu.VMEM(((rows + 2) * pitch, features), bf16),
        ],
        compiler_params=pltpu.CompilerParams(vmem_limit_bytes=VMEM_LIMIT),
        name="joining",
    )(
        first,
        above_far,
        above,
        reassembled,
        below,
        below_far,
        joining_weight,
        opening_weight,
        closing_weight,
    )


def on_device_line(
    tokens,
    query_weight,
    key_weight,
    value_weight,
    adapter_down_weight,
    query_adapter_up_weight,
    value_adapter_up_weight,
    query_norm_gain,
    key_norm_gain,
    output_weight,
    reassemble_weight,
    joining_kernel,
    opening_residual_kernel,
    closing_residual_kernel,
):
    place = lax.axis_index("tensor").astype(jnp.int32)
    images = lax.axis_size("dp")
    image = lax.axis_index("dp")
    rows, model_width = tokens.shape
    heads_width = output_weight.shape[0]
    send = lambda value, pairs: lax.ppermute(value, "tensor", pairs)
    after = lambda value, *others: lax.optimization_barrier((value, others))[0]

    rank = query_adapter_up_weight.shape[0]
    ups = (
        jnp.pad(query_adapter_up_weight, ((0, rank), (0, 0))),
        jnp.pad(value_adapter_up_weight, ((rank, 0), (0, 0))),
    )
    gains = (query_norm_gain.reshape(1, heads_width), key_norm_gain.reshape(1, heads_width))
    heads = lambda *parts, **kwargs: project(
        parts,
        (query_weight, key_weight, value_weight),
        adapter_down_weight,
        ups,
        gains,
        **kwargs,
    )

    cut = model_width // KEY_STEPS * (KEY_STEPS - LAST_STEPS)
    rest = dict(first=cut)
    inward, outward = [(0, 1), (3, 2)], [(1, 0), (2, 3)]

    (own,) = normalized_rows(tokens, (model_width,))
    up1 = send(own, [(0, 1), (1, 2), (2, 3)])
    down1 = send(own, [(1, 0), (2, 1), (3, 2)])
    (own_heads,) = heads(own)
    share = heads_width // images
    piece = lax.dynamic_slice_in_dim(output_weight, image * share, share, 0)
    piece = send(after(piece, own_heads), inward)
    share = reassemble_weight.shape[0] // images
    small = lax.dynamic_slice_in_dim(reassemble_weight, image * share, share, 0)
    small_end = send(after(small, own_heads), inward)

    up1, down1 = after((up1, down1), own_heads)
    up2 = send(up1, [(1, 2), (2, 3)])
    down2 = send(down1, [(2, 1), (1, 0)])
    before_heads, after_heads = heads(up1, down1)

    two = after(up2 + down2, before_heads, after_heads)
    partner_weight = lax.all_gather(after(piece, two), "dp", axis=0, tiled=True)
    two = (two[:, :cut], two[:, cut:])
    last = [send(part, outward) for part in two]
    small_two = send(after(jnp.stack([small, small_end]), up2, down2), [(1, 2), (2, 1)])
    two_sums = heads(two[0], final=False)
    (two_heads,) = heads(two[1], earlier=two_sums, **rest)
    last_sums = heads(after(last[0], two_heads), final=False)
    (last_heads,) = heads(last[1], earlier=last_sums, **rest)

    far, near, mine, edge = attention(
        place, own_heads, before_heads, after_heads, two_heads, last_heads
    )
    far_got = send(far, inward)
    near_got = send(near, inward)
    mine_got = send(edge, inward)

    held = jnp.stack([small, small_end, small_two[0], small_two[1]])
    three = send(after(jnp.stack([small, small_two[0], small_two[1]]), last[1]), outward)
    three, held = after((three, held), far)
    shares = jnp.where(
        place == 0,
        jnp.stack([small, three[0], three[1], three[2]]),
        jnp.where(
            place == 1,
            jnp.stack([held[1], held[0], held[2], held[3]]),
            jnp.where(
                place == 2,
                jnp.stack([held[3], held[2], held[0], held[1]]),
                jnp.stack([three[2], three[1], three[0], small]),
            ),
        ),
    )
    reassemble_full = lax.all_gather(shares, "dp", axis=1, tiled=True).reshape(
        model_width, reassemble_weight.shape[1]
    )

    edge = dot32(edge, output_weight).astype(bf16)
    edge = send(edge, outward)
    far = pair_sum(far, far_got, output_weight, partner_weight)
    far = send(far, [(1, 3), (2, 0)])
    near = pair_sum(near, near_got, output_weight, partner_weight)
    near = send(near, [(1, 2), (2, 1)])
    mine = (
        tokens.astype(f32) + dot32(mine, output_weight) + dot32(mine_got, partner_weight)
    )
    layer_out, reassembled = finish(mine, edge, far, near, reassemble_full)
    joined_map = joining(
        reassembled, joining_kernel, opening_residual_kernel, closing_residual_kernel
    )
    return (layer_out, joined_map)


def solution(mesh):
    body = on_device_line if mesh.shape["tensor"] == 4 else on_device
    return jax.shard_map(
        body,
        mesh=mesh,
        in_specs=(
            P(("dp", "tensor"), None),
            P(None, "tensor"),
            P(None, "tensor"),
            P(None, "tensor"),
            P(),
            P(None, "tensor"),
            P(None, "tensor"),
            P("tensor"),
            P("tensor"),
            P("tensor", None),
            P("tensor", None),
            P(),
            P(),
            P(),
        ),
        out_specs=(P(("dp", "tensor"), None), P(("dp", "tensor"), None, None)),
        check_vma=False,
    )
```

```python
import functools
import math

import jax
import jax.numpy as jnp
from jax import lax
from jax.experimental import pallas as pl
from jax.experimental.pallas import tpu as pltpu
from jax.sharding import PartitionSpec as P

HEAD_DIM = 128
MAP_W = 74


epsilon = 1e-06
adapter_scale = 2.0


def padded_2(value, sides, width):
    for axis, dim in sides:
        count, length = (lax.axis_size(axis), value.shape[dim])
        up = [(i, (i + 1) % count) for i in range(count - 1)]
        down = [(j, i) for i, j in up]
        last = lax.slice_in_dim(value, length - width, length, axis=dim)
        initial = lax.slice_in_dim(value, 0, width, axis=dim)
        before = lax.ppermute(last, axis, up)
        after = lax.ppermute(initial, axis, down)
        value = jnp.concatenate([before, value, after], axis=dim)
    return value


def normalize(values):
    average = jnp.mean(values, axis=-1, keepdims=True)
    centered = values - average
    variance = jnp.mean(centered * centered, axis=-1, keepdims=True)
    return centered * lax.rsqrt(variance + epsilon)


def conv_valid(padded, kernel):
    row_count = padded.shape[0] - 2
    col_count = padded.shape[1] - 2
    running = jnp.zeros((row_count, col_count, kernel.shape[3]), jnp.float32)
    for offset_row in range(3):
        for offset_col in range(3):
            window = padded[
                offset_row : offset_row + row_count, offset_col : offset_col + col_count, :
            ]
            running = running + jnp.einsum(
                "rwc,cf->rwf",
                window,
                kernel[offset_row, offset_col],
                preferred_element_type=jnp.float32,
            )
    return running


def pad_columns(field):
    return jnp.pad(field, ((0, 0), (1, 1), (0, 0)))


def extend_rows(field):
    return padded_2(field, (("tensor", 0),), 1)


def attend(
    normalized_input,
    query_weight,
    key_weight,
    value_weight,
    adapter_down_weight,
    query_adapter_up_weight,
    value_adapter_up_weight,
    query_norm_gain,
    key_norm_gain,
):
    reduced_rows = query_adapter_up_weight.shape[0]
    reduced_output = jnp.dot(
        normalized_input, adapter_down_weight, preferred_element_type=jnp.float32
    ).astype(jnp.bfloat16)
    query_matrix = jnp.dot(
        normalized_input, query_weight, preferred_element_type=jnp.float32
    ) + adapter_scale * jnp.dot(
        reduced_output[:, :reduced_rows],
        query_adapter_up_weight,
        preferred_element_type=jnp.float32,
    )
    key_rows = jnp.dot(normalized_input, key_weight, preferred_element_type=jnp.float32)
    value_matrix = (
        jnp.dot(normalized_input, value_weight, preferred_element_type=jnp.float32)
        + adapter_scale
        * jnp.dot(
            reduced_output[:, reduced_rows:],
            value_adapter_up_weight,
            preferred_element_type=jnp.float32,
        )
    ).astype(jnp.bfloat16)
    token_count = normalized_input.shape[0]
    head_count = query_weight.shape[1] // HEAD_DIM
    shape_heads = (token_count, head_count, HEAD_DIM)
    query_heads = (
        normalize(query_matrix.reshape(shape_heads))
        * (query_norm_gain.reshape(head_count, HEAD_DIM) / math.sqrt(HEAD_DIM))
    ).astype(jnp.bfloat16)
    key_heads = (
        normalize(key_rows.reshape(shape_heads)) * key_norm_gain.reshape(head_count, HEAD_DIM)
    ).astype(jnp.bfloat16)
    scores = jnp.einsum("qhd,khd->hqk", query_heads, key_heads, preferred_element_type=jnp.float32)
    raised = jnp.exp(scores)
    softmax_weights = (raised / jnp.sum(raised, axis=-1, keepdims=True)).astype(jnp.bfloat16)
    attended = jnp.einsum(
        "hqk,khd->qhd",
        softmax_weights,
        value_matrix.reshape(shape_heads),
        preferred_element_type=jnp.float32,
    )
    return attended.astype(jnp.bfloat16).reshape(token_count, head_count * HEAD_DIM)


def on_device(
    tokens,
    query_weight,
    key_weight,
    value_weight,
    adapter_down_weight,
    query_adapter_up_weight,
    value_adapter_up_weight,
    query_norm_gain,
    key_norm_gain,
    output_weight,
    reassemble_weight,
    joining_kernel,
    opening_residual_kernel,
    closing_residual_kernel,
):
    local_rows = tokens.shape[0]
    model_width = tokens.shape[1]
    everyone = lax.all_gather(tokens, "tensor", axis=0, tiled=True)
    normalized_input = normalize(everyone.astype(jnp.float32)).astype(jnp.bfloat16)
    attended = attend(
        normalized_input,
        query_weight,
        key_weight,
        value_weight,
        adapter_down_weight,
        query_adapter_up_weight,
        value_adapter_up_weight,
        query_norm_gain,
        key_norm_gain,
    )
    partials = jnp.dot(attended, output_weight, preferred_element_type=jnp.float32)
    column_sum = lax.psum_scatter(
        partials.astype(jnp.bfloat16), "tensor", scatter_dimension=1, tiled=True
    ).astype(jnp.float32)
    slice_width = model_width // lax.axis_size("tensor")
    own_columns = lax.dynamic_slice_in_dim(
        everyone, lax.axis_index("tensor") * slice_width, slice_width, 1
    )
    layer_columns = (own_columns.astype(jnp.float32) + column_sum).astype(jnp.bfloat16)
    layer_out = lax.all_to_all(layer_columns, "tensor", split_axis=0, concat_axis=1, tiled=True)
    reassembled = lax.psum_scatter(
        jnp.dot(layer_columns, reassemble_weight, preferred_element_type=jnp.float32).astype(
            jnp.bfloat16
        ),
        "tensor",
        scatter_dimension=0,
        tiled=True,
    )
    map_strip = reassembled.reshape(local_rows // MAP_W, MAP_W, reassemble_weight.shape[1])
    rimmed = padded_2(map_strip, (("tensor", 0),), 1)
    feature = conv_valid(pad_columns(rimmed), joining_kernel).astype(jnp.bfloat16)
    inner_field = jax.nn.relu(
        conv_valid(pad_columns(extend_rows(jax.nn.relu(feature))), opening_residual_kernel)
    ).astype(jnp.bfloat16)
    joined_map = (
        conv_valid(pad_columns(extend_rows(inner_field)), closing_residual_kernel)
        + feature.astype(jnp.float32)
    ).astype(jnp.bfloat16)
    return (layer_out, joined_map)


f32 = jnp.float32
bf16 = jnp.bfloat16
KEY_STEPS = 6
FINISH_STEPS = 4
PAIR_STEPS = 4
HEADS_STEP = 2
LAST_STEPS = 2
ROW_BLOCK = 80
VMEM_LIMIT = 56 * 1024 * 1024


def round_up(value, unit):
    return (value + unit - 1) // unit * unit


def dot32(a, b):
    return jnp.dot(a, b, preferred_element_type=f32)


def rows_kernel(tokens, *outs):
    normed = normalize(tokens[...].astype(f32)).astype(bf16)
    begin = 0
    for out in outs:
        out[...] = normed[:, begin : begin + out.shape[1]]
        begin += out.shape[1]


def normalized_rows(tokens, widths):
    rows, model_width = tokens.shape
    block = lambda width: pl.BlockSpec((ROW_BLOCK, width), lambda r: (r, 0))
    return pl.pallas_call(
        rows_kernel,
        grid=(pl.cdiv(rows, ROW_BLOCK),),
        in_specs=[block(model_width)],
        out_specs=[block(width) for width in widths],
        out_shape=[jax.ShapeDtypeStruct((rows, width), bf16) for width in widths],
        compiler_params=pltpu.CompilerParams(vmem_limit_bytes=VMEM_LIMIT),
        name="normalized_rows",
    )(tokens)


def project_kernel(count, cuts, given, final, *refs):
    pieces = len(cuts) - 1
    parts = refs[: count * pieces]
    refs = refs[count * pieces :]
    weights = refs[:3]
    down, query_up, value_up, query_gain, key_gain = refs[3:8]
    refs = refs[8:]
    earlier, refs = (refs[:2], refs[2:]) if given else (None, refs)
    outs, (totals, low) = refs[:-2], refs[-2:]
    step = pl.program_id(0)

    @pl.when(step == 0)
    def _():
        for i in range(count):
            for j in range(3):
                term = dot32(parts[i * pieces][...], weights[j][...])
                totals[i, j] = term + earlier[0][i, j] if given else term
            term = dot32(parts[i * pieces][...], down[...])
            low[i] = term + earlier[1][i] if given else term

    for p in range(pieces):

        @pl.when((step >= max(cuts[p], 1)) & (step < cuts[p + 1]))
        def _():
            for i in range(count):
                part = parts[i * pieces + p]
                for j in range(3):
                    totals[i, j] += dot32(part[...], weights[j][...])
                low[i] += dot32(part[...], down[...])

    @pl.when(step == pl.num_programs(0) - 1)
    def _():
        if not final:
            outs[0][...] = totals[...]
            outs[1][...] = low[...]
            return
        for i in range(count):
            reduced = low[i].astype(bf16)
            query = totals[i, 0] + adapter_scale * dot32(reduced, query_up[...])
            value = totals[i, 2] + adapter_scale * dot32(reduced, value_up[...])
            key = totals[i, 1]
            for h in range(query.shape[1] // HEAD_DIM):
                lanes = slice(h * HEAD_DIM, (h + 1) * HEAD_DIM)
                outs[i][0, :, lanes] = (
                    normalize(query[:, lanes]) * (query_gain[:, lanes] / math.sqrt(HEAD_DIM))
                ).astype(bf16)
                outs[i][1, :, lanes] = (
                    normalize(key[:, lanes]) * key_gain[:, lanes]
                ).astype(bf16)
            outs[i][2] = value.astype(bf16)


def project(parts, weights, down, ups, gains, first=0, earlier=(), final=True):
    count = len(parts)
    rows = parts[0][0].shape[0]
    model_width, width = weights[0].shape
    depth = model_width // KEY_STEPS
    cuts = [0]
    for piece in parts[0]:
        cuts.append(cuts[-1] + piece.shape[1] // depth)
    offset = first // depth
    rank = down.shape[1]
    whole = lambda *shape: pl.BlockSpec(shape, lambda k: (0,) * len(shape))
    piece_spec = lambda p: pl.BlockSpec(
        (rows, depth), lambda k: (0, jnp.clip(k - cuts[p], 0, cuts[p + 1] - cuts[p] - 1))
    )
    sums = [(count, 3, rows, width), (count, rows, rank)]
    results = [((3, rows, width), bf16)] * count if final else [(x, f32) for x in sums]
    result = pl.pallas_call(
        functools.partial(project_kernel, count, cuts, len(earlier) > 0, final),
        grid=(cuts[-1],),
        in_specs=[piece_spec(p) for p in range(len(cuts) - 1)] * count
        + [pl.BlockSpec((depth, width), lambda k: (k + offset, 0))] * 3
        + [pl.BlockSpec((depth, rank), lambda k: (k + offset, 0))]
        + [whole(rank, width)] * 2
        + [whole(1, width)] * 2
        + [whole(*x.shape) for x in earlier],
        out_specs=[whole(*shape) for shape, _ in results],
        out_shape=[jax.ShapeDtypeStruct(*x) for x in results],
        scratch_shapes=[pltpu.VMEM(shape, f32) for shape in sums],
        compiler_params=pltpu.CompilerParams(vmem_limit_bytes=VMEM_LIMIT),
        name="project",
    )(*(piece for block in parts for piece in block), *weights, down, *ups, *gains, *earlier)
    return result


def attention_kernel(rows, slot, place, *refs):
    blocks = refs[:5]
    outs = refs[5:9]
    query, key, value = refs[9:]
    where = place[0]

    @pl.when(pl.program_id(0) == 0)
    def _():
        for ref in (query, key, value):
            ref[...] = jnp.zeros_like(ref)
        lane = lax.broadcasted_iota(jnp.int32, (rows, HEAD_DIM), 1)
        ones = jnp.where(lane == 0, 1.0, 0.0).astype(bf16)
        for h in range(HEADS_STEP):
            for i in range(4):
                value[h, i * slot : i * slot + rows, HEAD_DIM:] = ones

    for j in range(3):
        own, before, after, two, last = (block.at[j] for block in blocks)

        def hold(i, ref):
            for h in range(HEADS_STEP):
                lanes = slice(h * HEAD_DIM, (h + 1) * HEAD_DIM)
                if j < 2:
                    (query, key)[j][h, i * slot : i * slot + rows] = ref[:, lanes]
                else:
                    value[h, i * slot : i * slot + rows, :HEAD_DIM] = ref[:, lanes]

        hold(0, own)
        hold(2, two)
        for i, end, other in ((1, 3, after), (3, 0, before)):
            pl.when(where == end)(functools.partial(hold, i, last))
            pl.when(where != end)(functools.partial(hold, i, other))

    inner = (where == 1) | (where == 2)
    far = jnp.where(inner, 2, jnp.where(where == 0, 3, 1))
    near = jnp.where(inner, jnp.where(where == 1, 1, 3), 2)
    edge = jnp.where((where == 0) | (where == 2), 1, 3)
    for asked, out in zip((far, near, 0, edge), outs):
        asked_rows = pl.ds(pl.multiple_of(asked * slot, slot), slot)
        for h in range(HEADS_STEP):
            scores = lax.dot_general(
                query[h, asked_rows],
                key[h],
                (((1,), (1,)), ((), ())),
                preferred_element_type=f32,
            )
            sums = dot32(jnp.exp(scores).astype(bf16), value[h])
            result = sums[:, :HEAD_DIM] / sums[:, HEAD_DIM : HEAD_DIM + 1]
            lanes = slice(h * HEAD_DIM, (h + 1) * HEAD_DIM)
            out[:, lanes] = result[:rows].astype(bf16)


def attention(place, *qkv):
    _, rows, width = qkv[0].shape
    slot = round_up(rows, 16)
    columns = HEADS_STEP * HEAD_DIM
    block = pl.BlockSpec((3, rows, columns), lambda h: (0, 0, h))
    return pl.pallas_call(
        functools.partial(attention_kernel, rows, slot),
        grid=(width // columns,),
        in_specs=[pl.BlockSpec(memory_space=pltpu.SMEM)] + [block] * 5,
        out_specs=[pl.BlockSpec((rows, columns), lambda h: (0, h))] * 4,
        out_shape=[jax.ShapeDtypeStruct((rows, width), bf16)] * 4,
        scratch_shapes=[
            pltpu.VMEM((HEADS_STEP, 4 * slot, HEAD_DIM), bf16),
            pltpu.VMEM((HEADS_STEP, 4 * slot, HEAD_DIM), bf16),
            pltpu.VMEM((HEADS_STEP, 4 * slot, 2 * HEAD_DIM), bf16),
        ],
        compiler_params=pltpu.CompilerParams(vmem_limit_bytes=VMEM_LIMIT),
        name="attention",
    )(place.reshape(1), *qkv)


def own_sums_kernel(rows, slot, edge, mine, tokens, weight, edge_out, mine_out, held):
    @pl.when(pl.program_id(0) == 0)
    def _():
        held[...] = jnp.zeros_like(held)
        held[0:rows] = edge[...]
        held[slot : slot + rows] = mine[...]

    result = dot32(held[...], weight[...])
    edge_out[...] = result[:rows].astype(bf16)
    mine_out[...] = tokens[...].astype(f32) + result[slot : slot + rows]


def own_sums(edge, mine, tokens, weight):
    rows, width = mine.shape
    model_width = weight.shape[1]
    slot = round_up(rows, 16)
    columns = model_width // PAIR_STEPS
    operand = pl.BlockSpec((rows, width), lambda c: (0, 0))
    block = pl.BlockSpec((rows, columns), lambda c: (0, c))
    return pl.pallas_call(
        functools.partial(own_sums_kernel, rows, slot),
        grid=(PAIR_STEPS,),
        in_specs=[operand] * 2 + [block, pl.BlockSpec((width, columns), lambda c: (0, c))],
        out_specs=[block] * 2,
        out_shape=[
            jax.ShapeDtypeStruct((rows, model_width), bf16),
            jax.ShapeDtypeStruct((rows, model_width), f32),
        ],
        scratch_shapes=[pltpu.VMEM((2 * slot, width), bf16)],
        compiler_params=pltpu.CompilerParams(vmem_limit_bytes=VMEM_LIMIT),
        name="own_sums",
    )(edge, mine, tokens, weight)


def pair_sums_kernel(rows, slot, far, near, far_got, near_got, own, got, *refs):
    far_out, near_out, held, held_got = refs

    @pl.when(pl.program_id(0) == 0)
    def _():
        for ref, first, second in ((held, far, near), (held_got, far_got, near_got)):
            ref[...] = jnp.zeros_like(ref)
            ref[0:rows] = first[...]
            ref[slot : slot + rows] = second[...]

    result = dot32(held[...], own[...]) + dot32(held_got[...], got[...])
    far_out[...] = result[:rows].astype(bf16)
    near_out[...] = result[slot : slot + rows].astype(bf16)


def pair_sums(far, near, far_got, near_got, own, got, half):
    rows, width = far.shape
    model_width = own.shape[1]
    slot = round_up(rows, 16)
    columns = model_width // PAIR_STEPS
    steps = PAIR_STEPS // 2
    operand = pl.BlockSpec((rows, width), lambda c: (0, 0))
    weight = pl.BlockSpec((width, columns), lambda c: (0, c + half * steps))
    block = pl.BlockSpec((rows, columns), lambda c: (0, c))
    return pl.pallas_call(
        functools.partial(pair_sums_kernel, rows, slot),
        grid=(steps,),
        in_specs=[operand] * 4 + [weight] * 2,
        out_specs=[block] * 2,
        out_shape=[jax.ShapeDtypeStruct((rows, model_width // 2), bf16)] * 2,
        scratch_shapes=[pltpu.VMEM((2 * slot, width), bf16)] * 2,
        compiler_params=pltpu.CompilerParams(vmem_limit_bytes=VMEM_LIMIT),
        name="pair_sums",
    )(far, near, far_got, near_got, own, got)


def add_kernel(mine, other, weight, out):
    out[...] = mine[...] + dot32(other[...], weight[...])


def add_sums(mine, other, weight):
    rows, width = other.shape
    model_width = weight.shape[1]
    columns = model_width // PAIR_STEPS
    block = pl.BlockSpec((rows, columns), lambda c: (0, c))
    return pl.pallas_call(
        add_kernel,
        grid=(PAIR_STEPS,),
        in_specs=[
            block,
            pl.BlockSpec((rows, width), lambda c: (0, 0)),
            pl.BlockSpec((width, columns), lambda c: (0, c)),
        ],
        out_specs=block,
        out_shape=jax.ShapeDtypeStruct((rows, model_width), f32),
        compiler_params=pltpu.CompilerParams(vmem_limit_bytes=VMEM_LIMIT),
        name="add_sums",
    )(mine, other, weight)


def finish_kernel(half, mine, edge, far, near, weight, *refs):
    layer_out, reassembled, total = refs[-3:]
    step = pl.program_id(0)
    layer = (
        mine[...] + edge[...].astype(f32) + far[...].astype(f32) + near[...].astype(f32)
    ).astype(bf16)
    layer_out[...] = layer
    term = dot32(layer, weight[...])

    @pl.when(step == 0)
    def _():
        total[...] = term + refs[0][...] if half else term

    @pl.when(step > 0)
    def _():
        total[...] += term

    @pl.when(step == pl.num_programs(0) - 1)
    def _():
        if half:
            rows = reassembled.shape[1]
            for r in range(reassembled.shape[0]):
                reassembled[r] = total[r * rows : (r + 1) * rows].astype(bf16)
        else:
            reassembled[...] = total[...]


def finish(mine, edge, far, near, weight, half, earlier=()):
    rows, model_width = mine.shape
    channels = weight.shape[1]
    depth = model_width // FINISH_STEPS
    steps = FINISH_STEPS // 2
    wide = pl.BlockSpec((rows, depth), lambda k: (0, k + half * steps))
    block = pl.BlockSpec((rows, depth), lambda k: (0, k))
    shape = (rows // MAP_W, MAP_W, channels) if half else (rows, channels)
    whole = lambda *x: pl.BlockSpec(x, lambda k: (0,) * len(x))
    return pl.pallas_call(
        functools.partial(finish_kernel, half),
        grid=(steps,),
        in_specs=[wide, wide, block, block]
        + [pl.BlockSpec((depth, channels), lambda k: (k + half * steps, 0))]
        + ([whole(rows, channels), pl.BlockSpec(memory_space=pl.ANY)] if half else []),
        out_specs=[wide, whole(*shape)],
        out_shape=[
            jax.ShapeDtypeStruct((rows, model_width), bf16),
            jax.ShapeDtypeStruct(shape, bf16 if half else f32),
        ],
        scratch_shapes=[pltpu.VMEM((rows, channels), f32)],
        input_output_aliases={6: 0} if half else {},
        compiler_params=pltpu.CompilerParams(vmem_limit_bytes=VMEM_LIMIT),
        name="finish",
    )(mine, edge, far, near, weight, *earlier)


def joining_kernel_body(total_rows, pitch, first, *refs):
    pieces = refs[:5]
    joining, opening, closing, out, field, feature, inner = refs[5:]
    field[...] = jnp.zeros_like(field)
    place = 0
    for piece in pieces:
        for r in range(piece.shape[0]):
            field[place * pitch : place * pitch + MAP_W] = piece[r]
            place += 1

    def conv(source, kernel):
        size = source.shape[0] - 2 * pitch
        sums = []
        for b in range(3):
            running = None
            for a in range(3):
                term = dot32(source[a * pitch : a * pitch + size], kernel[a, b])
                running = term if running is None else running + term
            sums.append(running)
        return sums[1] + pltpu.roll(sums[0], 1, 0) + pltpu.roll(sums[2], size - 1, 0)

    def masked(values, margin):
        size, channels = values.shape
        shape = (size // pitch, pitch, channels)
        row = lax.broadcasted_iota(jnp.int32, shape, 0) + (first[0] - margin)
        column = lax.broadcasted_iota(jnp.int32, shape, 1)
        keep = (row >= 0) & (row < total_rows) & (column < MAP_W)
        return jnp.where(keep, values.reshape(shape), 0.0).reshape(size, channels)

    feature[...] = masked(conv(field, joining), 2).astype(bf16)
    rectified = jnp.maximum(feature[...], 0)
    inner[...] = masked(jax.nn.relu(conv(rectified, opening)), 1).astype(bf16)
    rows = out.shape[0]
    result = conv(inner, closing) + feature[2 * pitch : (2 + rows) * pitch].astype(f32)
    for r in range(rows):
        out[r] = result[r * pitch : r * pitch + MAP_W].astype(bf16)


def joining(reassembled, joining_weight, opening_weight, closing_weight):
    count = lax.axis_size("tensor")
    place = lax.axis_index("tensor")
    rows, _, channels = reassembled.shape
    features = joining_weight.shape[3]
    send = lambda value, pairs: lax.ppermute(value, "tensor", pairs)
    above = send(reassembled, [(i, i + 1) for i in range(count - 1)])
    below = send(reassembled, [(i + 1, i) for i in range(count - 1)])
    edge = jnp.where(place < 2, reassembled[rows - 1 :], reassembled[:1])
    edge = send(edge, [(0, 2), (1, 3), (2, 0), (3, 1)])
    above_far = jnp.where(place >= 2, edge, 0)
    below_far = jnp.where(place < 2, edge, 0)
    pitch = round_up(MAP_W + 1, 16)
    first = (place * rows).astype(jnp.int32).reshape(1)
    return pl.pallas_call(
        functools.partial(joining_kernel_body, count * rows, pitch),
        in_specs=[pl.BlockSpec(memory_space=pltpu.SMEM)]
        + [pl.BlockSpec(memory_space=pltpu.VMEM)] * 8,
        out_specs=pl.BlockSpec(memory_space=pltpu.VMEM),
        out_shape=jax.ShapeDtypeStruct((rows, MAP_W, features), bf16),
        scratch_shapes=[
            pltpu.VMEM(((rows + 6) * pitch, channels), bf16),
            pltpu.VMEM(((rows + 4) * pitch, features), bf16),
            pltpu.VMEM(((rows + 2) * pitch, features), bf16),
        ],
        compiler_params=pltpu.CompilerParams(vmem_limit_bytes=VMEM_LIMIT),
        name="joining",
    )(
        first,
        above_far,
        above,
        reassembled,
        below,
        below_far,
        joining_weight,
        opening_weight,
        closing_weight,
    )


def on_device_line(
    tokens,
    query_weight,
    key_weight,
    value_weight,
    adapter_down_weight,
    query_adapter_up_weight,
    value_adapter_up_weight,
    query_norm_gain,
    key_norm_gain,
    output_weight,
    reassemble_weight,
    joining_kernel,
    opening_residual_kernel,
    closing_residual_kernel,
):
    place = lax.axis_index("tensor").astype(jnp.int32)
    images = lax.axis_size("dp")
    image = lax.axis_index("dp")
    rows, model_width = tokens.shape
    heads_width = output_weight.shape[0]
    send = lambda value, pairs: lax.ppermute(value, "tensor", pairs)
    after = lambda value, *others: lax.optimization_barrier((value, others))[0]

    rank = query_adapter_up_weight.shape[0]
    ups = (
        jnp.pad(query_adapter_up_weight, ((0, rank), (0, 0))),
        jnp.pad(value_adapter_up_weight, ((rank, 0), (0, 0))),
    )
    gains = (query_norm_gain.reshape(1, heads_width), key_norm_gain.reshape(1, heads_width))
    heads = lambda *parts, **kwargs: project(
        parts,
        (query_weight, key_weight, value_weight),
        adapter_down_weight,
        ups,
        gains,
        **kwargs,
    )

    cut = model_width // KEY_STEPS * (KEY_STEPS - LAST_STEPS)
    rest = dict(first=cut)
    inward, outward = [(0, 1), (3, 2)], [(1, 0), (2, 3)]

    (own,) = normalized_rows(tokens, (model_width,))
    up1 = send(own, [(0, 1), (1, 2), (2, 3)])
    down1 = send(own, [(1, 0), (2, 1), (3, 2)])
    (own_heads,) = heads([own])
    share = heads_width // images
    piece = lax.dynamic_slice_in_dim(output_weight, image * share, share, 0)
    piece = send(after(piece, own_heads), inward)
    share = reassemble_weight.shape[0] // images
    small = lax.dynamic_slice_in_dim(reassemble_weight, image * share, share, 0)
    small_end = send(after(small, own_heads), inward)

    up1, down1 = after((up1, down1), own_heads)
    up2 = send(up1, [(1, 2), (2, 3)])
    down2 = send(down1, [(2, 1), (1, 0)])
    before_heads, after_heads = heads([up1], [down1])

    two = after(up2 + down2, before_heads, after_heads)
    partner_weight = lax.all_gather(after(piece, two), "dp", axis=0, tiled=True)
    two = (two[:, :cut], two[:, cut:])
    last = [send(two[0], outward)]
    small_two = send(after(jnp.stack([small, small_end]), up2, down2), [(1, 2), (2, 1)])
    two_sums = heads([two[0]], final=False)
    last.append(send(after(two[1], two_sums), outward))
    (two_heads,) = heads([two[1]], earlier=two_sums, **rest)
    last_sums = heads([after(last[0], two_heads)], final=False)
    (last_heads,) = heads([last[1]], earlier=last_sums, **rest)

    three = jnp.stack([small, small_two[0], small_two[1]])
    three = send(after(three, last_heads), outward)

    far, near, mine, edge = attention(
        place, own_heads, before_heads, after_heads, two_heads, last_heads
    )
    far_got = send(far, inward)
    near_got = send(near, inward)
    edge_rows = edge
    edge, mine = own_sums(edge, mine, tokens, output_weight)
    far_got, near_got = after((far_got, near_got), edge)
    edge = send(after(edge, far_got), outward)
    parts = []
    for half in range(2):
        if half == 1:
            far = after(far, sums)
        sums = pair_sums(far, near, far_got, near_got, output_weight, partner_weight, half)
        parts.append((send(sums[0], [(1, 3), (2, 0)]), send(sums[1], [(1, 2), (2, 1)])))
        if half == 0:
            mine_got = send(after(edge_rows, parts[0][0]), inward)
    small, small_end, small_two, three = after((small, small_end, small_two, three), far_got)
    mine = add_sums(mine, mine_got, partner_weight)

    held = jnp.stack([small, small_end, small_two[0], small_two[1]])
    shares = jnp.where(
        place == 0,
        jnp.stack([small, three[0], three[1], three[2]]),
        jnp.where(
            place == 1,
            jnp.stack([held[1], held[0], held[2], held[3]]),
            jnp.where(
                place == 2,
                jnp.stack([held[3], held[2], held[0], held[1]]),
                jnp.stack([three[2], three[1], three[0], small]),
            ),
        ),
    )
    reassemble_full = lax.all_gather(shares, "dp", axis=1, tiled=True).reshape(
        model_width, reassemble_weight.shape[1]
    )

    layer_out, sums = finish(mine, edge, *parts[0], reassemble_full, 0)
    layer_out, reassembled = finish(mine, edge, *parts[1], reassemble_full, 1, (sums, layer_out))
    joined_map = joining(
        reassembled, joining_kernel, opening_residual_kernel, closing_residual_kernel
    )
    return (layer_out, joined_map)


def solution(mesh):
    body = on_device_line if mesh.shape["tensor"] == 4 else on_device
    return jax.shard_map(
        body,
        mesh=mesh,
        in_specs=(
            P(("dp", "tensor"), None),
            P(None, "tensor"),
            P(None, "tensor"),
            P(None, "tensor"),
            P(),
            P(None, "tensor"),
            P(None, "tensor"),
            P("tensor"),
            P("tensor"),
            P("tensor", None),
            P("tensor", None),
            P(),
            P(),
            P(),
        ),
        out_specs=(P(("dp", "tensor"), None), P(("dp", "tensor"), None, None)),
        check_vma=False,
    )
```

```python
import functools
import math

import jax
import jax.numpy as jnp
from jax import lax
from jax.experimental import pallas as pl
from jax.experimental.pallas import tpu as pltpu
from jax.sharding import PartitionSpec as P

HEAD_DIM = 128
MAP_W = 74


epsilon = 1e-06
adapter_scale = 2.0


def padded_2(value, sides, width):
    for axis, dim in sides:
        count, length = (lax.axis_size(axis), value.shape[dim])
        up = [(i, (i + 1) % count) for i in range(count - 1)]
        down = [(j, i) for i, j in up]
        last = lax.slice_in_dim(value, length - width, length, axis=dim)
        initial = lax.slice_in_dim(value, 0, width, axis=dim)
        before = lax.ppermute(last, axis, up)
        after = lax.ppermute(initial, axis, down)
        value = jnp.concatenate([before, value, after], axis=dim)
    return value


def normalize(values):
    average = jnp.mean(values, axis=-1, keepdims=True)
    centered = values - average
    variance = jnp.mean(centered * centered, axis=-1, keepdims=True)
    return centered * lax.rsqrt(variance + epsilon)


def conv_valid(padded, kernel):
    row_count = padded.shape[0] - 2
    col_count = padded.shape[1] - 2
    running = jnp.zeros((row_count, col_count, kernel.shape[3]), jnp.float32)
    for offset_row in range(3):
        for offset_col in range(3):
            window = padded[
                offset_row : offset_row + row_count, offset_col : offset_col + col_count, :
            ]
            running = running + jnp.einsum(
                "rwc,cf->rwf",
                window,
                kernel[offset_row, offset_col],
                preferred_element_type=jnp.float32,
            )
    return running


def pad_columns(field):
    return jnp.pad(field, ((0, 0), (1, 1), (0, 0)))


def extend_rows(field):
    return padded_2(field, (("tensor", 0),), 1)


def attend(
    normalized_input,
    query_weight,
    key_weight,
    value_weight,
    adapter_down_weight,
    query_adapter_up_weight,
    value_adapter_up_weight,
    query_norm_gain,
    key_norm_gain,
):
    reduced_rows = query_adapter_up_weight.shape[0]
    reduced_output = jnp.dot(
        normalized_input, adapter_down_weight, preferred_element_type=jnp.float32
    ).astype(jnp.bfloat16)
    query_matrix = jnp.dot(
        normalized_input, query_weight, preferred_element_type=jnp.float32
    ) + adapter_scale * jnp.dot(
        reduced_output[:, :reduced_rows],
        query_adapter_up_weight,
        preferred_element_type=jnp.float32,
    )
    key_rows = jnp.dot(normalized_input, key_weight, preferred_element_type=jnp.float32)
    value_matrix = (
        jnp.dot(normalized_input, value_weight, preferred_element_type=jnp.float32)
        + adapter_scale
        * jnp.dot(
            reduced_output[:, reduced_rows:],
            value_adapter_up_weight,
            preferred_element_type=jnp.float32,
        )
    ).astype(jnp.bfloat16)
    token_count = normalized_input.shape[0]
    head_count = query_weight.shape[1] // HEAD_DIM
    shape_heads = (token_count, head_count, HEAD_DIM)
    query_heads = (
        normalize(query_matrix.reshape(shape_heads))
        * (query_norm_gain.reshape(head_count, HEAD_DIM) / math.sqrt(HEAD_DIM))
    ).astype(jnp.bfloat16)
    key_heads = (
        normalize(key_rows.reshape(shape_heads)) * key_norm_gain.reshape(head_count, HEAD_DIM)
    ).astype(jnp.bfloat16)
    scores = jnp.einsum("qhd,khd->hqk", query_heads, key_heads, preferred_element_type=jnp.float32)
    raised = jnp.exp(scores)
    softmax_weights = (raised / jnp.sum(raised, axis=-1, keepdims=True)).astype(jnp.bfloat16)
    attended = jnp.einsum(
        "hqk,khd->qhd",
        softmax_weights,
        value_matrix.reshape(shape_heads),
        preferred_element_type=jnp.float32,
    )
    return attended.astype(jnp.bfloat16).reshape(token_count, head_count * HEAD_DIM)


def on_device(
    tokens,
    query_weight,
    key_weight,
    value_weight,
    adapter_down_weight,
    query_adapter_up_weight,
    value_adapter_up_weight,
    query_norm_gain,
    key_norm_gain,
    output_weight,
    reassemble_weight,
    joining_kernel,
    opening_residual_kernel,
    closing_residual_kernel,
):
    local_rows = tokens.shape[0]
    model_width = tokens.shape[1]
    everyone = lax.all_gather(tokens, "tensor", axis=0, tiled=True)
    normalized_input = normalize(everyone.astype(jnp.float32)).astype(jnp.bfloat16)
    attended = attend(
        normalized_input,
        query_weight,
        key_weight,
        value_weight,
        adapter_down_weight,
        query_adapter_up_weight,
        value_adapter_up_weight,
        query_norm_gain,
        key_norm_gain,
    )
    partials = jnp.dot(attended, output_weight, preferred_element_type=jnp.float32)
    column_sum = lax.psum_scatter(
        partials.astype(jnp.bfloat16), "tensor", scatter_dimension=1, tiled=True
    ).astype(jnp.float32)
    slice_width = model_width // lax.axis_size("tensor")
    own_columns = lax.dynamic_slice_in_dim(
        everyone, lax.axis_index("tensor") * slice_width, slice_width, 1
    )
    layer_columns = (own_columns.astype(jnp.float32) + column_sum).astype(jnp.bfloat16)
    layer_out = lax.all_to_all(layer_columns, "tensor", split_axis=0, concat_axis=1, tiled=True)
    reassembled = lax.psum_scatter(
        jnp.dot(layer_columns, reassemble_weight, preferred_element_type=jnp.float32).astype(
            jnp.bfloat16
        ),
        "tensor",
        scatter_dimension=0,
        tiled=True,
    )
    map_strip = reassembled.reshape(local_rows // MAP_W, MAP_W, reassemble_weight.shape[1])
    rimmed = padded_2(map_strip, (("tensor", 0),), 1)
    feature = conv_valid(pad_columns(rimmed), joining_kernel).astype(jnp.bfloat16)
    inner_field = jax.nn.relu(
        conv_valid(pad_columns(extend_rows(jax.nn.relu(feature))), opening_residual_kernel)
    ).astype(jnp.bfloat16)
    joined_map = (
        conv_valid(pad_columns(extend_rows(inner_field)), closing_residual_kernel)
        + feature.astype(jnp.float32)
    ).astype(jnp.bfloat16)
    return (layer_out, joined_map)


f32 = jnp.float32
bf16 = jnp.bfloat16
KEY_STEPS = 6
FINISH_STEPS = 4
PAIR_STEPS = 4
EDGE_STEPS = 4
HEADS_STEP = 2
LAST_STEPS = 2
ROW_BLOCK = 80
VMEM_LIMIT = 56 * 1024 * 1024


def round_up(value, unit):
    return (value + unit - 1) // unit * unit


def dot32(a, b):
    return jnp.dot(a, b, preferred_element_type=f32)


def rows_kernel(tokens, *outs):
    normed = normalize(tokens[...].astype(f32)).astype(bf16)
    begin = 0
    for out in outs:
        out[...] = normed[:, begin : begin + out.shape[1]]
        begin += out.shape[1]


def normalized_rows(tokens, widths):
    rows, model_width = tokens.shape
    block = lambda width: pl.BlockSpec((ROW_BLOCK, width), lambda r: (r, 0))
    return pl.pallas_call(
        rows_kernel,
        grid=(pl.cdiv(rows, ROW_BLOCK),),
        in_specs=[block(model_width)],
        out_specs=[block(width) for width in widths],
        out_shape=[jax.ShapeDtypeStruct((rows, width), bf16) for width in widths],
        compiler_params=pltpu.CompilerParams(vmem_limit_bytes=VMEM_LIMIT),
        name="normalized_rows",
    )(tokens)


def project_kernel(count, cuts, given, final, *refs):
    pieces = len(cuts) - 1
    parts = refs[: count * pieces]
    refs = refs[count * pieces :]
    weights = refs[:3]
    down, query_up, value_up, query_gain, key_gain = refs[3:8]
    refs = refs[8:]
    earlier, refs = (refs[:2], refs[2:]) if given else (None, refs)
    outs, (totals, low) = refs[:-2], refs[-2:]
    step = pl.program_id(0)

    @pl.when(step == 0)
    def _():
        for i in range(count):
            for j in range(3):
                term = dot32(parts[i * pieces][...], weights[j][...])
                totals[i, j] = term + earlier[0][i, j] if given else term
            term = dot32(parts[i * pieces][...], down[...])
            low[i] = term + earlier[1][i] if given else term

    for p in range(pieces):

        @pl.when((step >= max(cuts[p], 1)) & (step < cuts[p + 1]))
        def _():
            for i in range(count):
                part = parts[i * pieces + p]
                for j in range(3):
                    totals[i, j] += dot32(part[...], weights[j][...])
                low[i] += dot32(part[...], down[...])

    @pl.when(step == pl.num_programs(0) - 1)
    def _():
        if not final:
            outs[0][...] = totals[...]
            outs[1][...] = low[...]
            return
        for i in range(count):
            reduced = low[i].astype(bf16)
            query = totals[i, 0] + adapter_scale * dot32(reduced, query_up[...])
            value = totals[i, 2] + adapter_scale * dot32(reduced, value_up[...])
            key = totals[i, 1]
            for h in range(query.shape[1] // HEAD_DIM):
                lanes = slice(h * HEAD_DIM, (h + 1) * HEAD_DIM)
                outs[i][0, :, lanes] = (
                    normalize(query[:, lanes]) * (query_gain[:, lanes] / math.sqrt(HEAD_DIM))
                ).astype(bf16)
                outs[i][1, :, lanes] = (
                    normalize(key[:, lanes]) * key_gain[:, lanes]
                ).astype(bf16)
            outs[i][2] = value.astype(bf16)


def project(parts, weights, down, ups, gains, first=0, earlier=(), final=True):
    count = len(parts)
    rows = parts[0][0].shape[0]
    model_width, width = weights[0].shape
    depth = model_width // KEY_STEPS
    cuts = [0]
    for piece in parts[0]:
        cuts.append(cuts[-1] + piece.shape[1] // depth)
    offset = first // depth
    rank = down.shape[1]
    whole = lambda *shape: pl.BlockSpec(shape, lambda k: (0,) * len(shape))
    piece_spec = lambda p: pl.BlockSpec(
        (rows, depth), lambda k: (0, jnp.clip(k - cuts[p], 0, cuts[p + 1] - cuts[p] - 1))
    )
    sums = [(count, 3, rows, width), (count, rows, rank)]
    results = [((3, rows, width), bf16)] * count if final else [(x, f32) for x in sums]
    result = pl.pallas_call(
        functools.partial(project_kernel, count, cuts, len(earlier) > 0, final),
        grid=(cuts[-1],),
        in_specs=[piece_spec(p) for p in range(len(cuts) - 1)] * count
        + [pl.BlockSpec((depth, width), lambda k: (k + offset, 0))] * 3
        + [pl.BlockSpec((depth, rank), lambda k: (k + offset, 0))]
        + [whole(rank, width)] * 2
        + [whole(1, width)] * 2
        + [whole(*x.shape) for x in earlier],
        out_specs=[whole(*shape) for shape, _ in results],
        out_shape=[jax.ShapeDtypeStruct(*x) for x in results],
        scratch_shapes=[pltpu.VMEM(shape, f32) for shape in sums],
        compiler_params=pltpu.CompilerParams(vmem_limit_bytes=VMEM_LIMIT),
        name="project",
    )(*(piece for block in parts for piece in block), *weights, down, *ups, *gains, *earlier)
    return result


def attention_kernel(rows, slot, place, *refs):
    blocks = refs[:5]
    outs = refs[5:9]
    query, key, value = refs[9:]
    where = place[0]

    @pl.when(pl.program_id(0) == 0)
    def _():
        for ref in (query, key, value):
            ref[...] = jnp.zeros_like(ref)
        lane = lax.broadcasted_iota(jnp.int32, (rows, HEAD_DIM), 1)
        ones = jnp.where(lane == 0, 1.0, 0.0).astype(bf16)
        for h in range(HEADS_STEP):
            for i in range(4):
                value[h, i * slot : i * slot + rows, HEAD_DIM:] = ones

    for j in range(3):
        own, before, after, two, last = (block.at[j] for block in blocks)

        def hold(i, ref):
            for h in range(HEADS_STEP):
                lanes = slice(h * HEAD_DIM, (h + 1) * HEAD_DIM)
                if j < 2:
                    (query, key)[j][h, i * slot : i * slot + rows] = ref[:, lanes]
                else:
                    value[h, i * slot : i * slot + rows, :HEAD_DIM] = ref[:, lanes]

        hold(0, own)
        hold(2, two)
        for i, end, other in ((1, 3, after), (3, 0, before)):
            pl.when(where == end)(functools.partial(hold, i, last))
            pl.when(where != end)(functools.partial(hold, i, other))

    inner = (where == 1) | (where == 2)
    far = jnp.where(inner, 2, jnp.where(where == 0, 3, 1))
    near = jnp.where(inner, jnp.where(where == 1, 1, 3), 2)
    edge = jnp.where((where == 0) | (where == 2), 1, 3)
    for asked, out in zip((far, near, 0, edge), outs):
        asked_rows = pl.ds(pl.multiple_of(asked * slot, slot), slot)
        for h in range(HEADS_STEP):
            scores = lax.dot_general(
                query[h, asked_rows],
                key[h],
                (((1,), (1,)), ((), ())),
                preferred_element_type=f32,
            )
            sums = dot32(jnp.exp(scores).astype(bf16), value[h])
            result = sums[:, :HEAD_DIM] / sums[:, HEAD_DIM : HEAD_DIM + 1]
            lanes = slice(h * HEAD_DIM, (h + 1) * HEAD_DIM)
            out[:, lanes] = result[:rows].astype(bf16)


def attention(place, *qkv):
    _, rows, width = qkv[0].shape
    slot = round_up(rows, 16)
    columns = HEADS_STEP * HEAD_DIM
    block = pl.BlockSpec((3, rows, columns), lambda h: (0, 0, h))
    return pl.pallas_call(
        functools.partial(attention_kernel, rows, slot),
        grid=(width // columns,),
        in_specs=[pl.BlockSpec(memory_space=pltpu.SMEM)] + [block] * 5,
        out_specs=[pl.BlockSpec((rows, columns), lambda h: (0, h))] * 4,
        out_shape=[jax.ShapeDtypeStruct((rows, width), bf16)] * 4,
        scratch_shapes=[
            pltpu.VMEM((HEADS_STEP, 4 * slot, HEAD_DIM), bf16),
            pltpu.VMEM((HEADS_STEP, 4 * slot, HEAD_DIM), bf16),
            pltpu.VMEM((HEADS_STEP, 4 * slot, 2 * HEAD_DIM), bf16),
        ],
        compiler_params=pltpu.CompilerParams(vmem_limit_bytes=VMEM_LIMIT),
        name="attention",
    )(place.reshape(1), *qkv)


def edge_kernel(edge, weight, out):
    out[...] = dot32(edge[...], weight[...]).astype(bf16)


def edge_sums(edge, weight):
    rows, width = edge.shape
    model_width = weight.shape[1]
    columns = model_width // EDGE_STEPS
    return pl.pallas_call(
        edge_kernel,
        grid=(EDGE_STEPS,),
        in_specs=[
            pl.BlockSpec((rows, width), lambda c: (0, 0)),
            pl.BlockSpec((width, columns), lambda c: (0, c)),
        ],
        out_specs=pl.BlockSpec((rows, columns), lambda c: (0, c)),
        out_shape=jax.ShapeDtypeStruct((rows, model_width), bf16),
        compiler_params=pltpu.CompilerParams(vmem_limit_bytes=VMEM_LIMIT),
        name="edge_sums",
    )(edge, weight)


def pair_sums_kernel(rows, slot, far, near, far_got, near_got, own, got, *refs):
    far_out, near_out, held, held_got = refs

    @pl.when(pl.program_id(0) == 0)
    def _():
        for ref, first, second in ((held, far, near), (held_got, far_got, near_got)):
            ref[...] = jnp.zeros_like(ref)
            ref[0:rows] = first[...]
            ref[slot : slot + rows] = second[...]

    result = dot32(held[...], own[...]) + dot32(held_got[...], got[...])
    far_out[...] = result[:rows].astype(bf16)
    near_out[...] = result[slot : slot + rows].astype(bf16)


def pair_sums(far, near, far_got, near_got, own, got, half):
    rows, width = far.shape
    model_width = own.shape[1]
    slot = round_up(rows, 16)
    columns = model_width // PAIR_STEPS
    steps = PAIR_STEPS // 2
    operand = pl.BlockSpec((rows, width), lambda c: (0, 0))
    weight = pl.BlockSpec((width, columns), lambda c: (0, c + half * steps))
    block = pl.BlockSpec((rows, columns), lambda c: (0, c))
    return pl.pallas_call(
        functools.partial(pair_sums_kernel, rows, slot),
        grid=(steps,),
        in_specs=[operand] * 4 + [weight] * 2,
        out_specs=[block] * 2,
        out_shape=[jax.ShapeDtypeStruct((rows, model_width // 2), bf16)] * 2,
        scratch_shapes=[pltpu.VMEM((2 * slot, width), bf16)] * 2,
        compiler_params=pltpu.CompilerParams(vmem_limit_bytes=VMEM_LIMIT),
        name="pair_sums",
    )(far, near, far_got, near_got, own, got)


def own_kernel(tokens, mine, other, own, got, out):
    out[...] = tokens[...].astype(f32) + (
        dot32(mine[...], own[...]) + dot32(other[...], got[...])
    )


def own_sums(tokens, mine, other, own, got):
    rows, width = mine.shape
    model_width = own.shape[1]
    columns = model_width // PAIR_STEPS
    operand = pl.BlockSpec((rows, width), lambda c: (0, 0))
    weight = pl.BlockSpec((width, columns), lambda c: (0, c))
    block = pl.BlockSpec((rows, columns), lambda c: (0, c))
    return pl.pallas_call(
        own_kernel,
        grid=(PAIR_STEPS,),
        in_specs=[block, operand, operand, weight, weight],
        out_specs=block,
        out_shape=jax.ShapeDtypeStruct((rows, model_width), f32),
        compiler_params=pltpu.CompilerParams(vmem_limit_bytes=VMEM_LIMIT),
        name="own_sums",
    )(tokens, mine, other, own, got)


def finish_kernel(half, mine, edge, far, near, weight, *refs):
    if half:
        place, earlier, _, layer_out, reassembled, far_row, total = refs
    else:
        layer_out, reassembled, total = refs
    step = pl.program_id(0)
    layer = (
        mine[...] + edge[...].astype(f32) + far[...].astype(f32) + near[...].astype(f32)
    ).astype(bf16)
    layer_out[...] = layer
    term = dot32(layer, weight[...])

    @pl.when(step == 0)
    def _():
        total[...] = term + earlier[...] if half else term

    @pl.when(step > 0)
    def _():
        total[...] += term

    @pl.when(step == pl.num_programs(0) - 1)
    def _():
        if half:
            rows = reassembled.shape[1]
            count = reassembled.shape[0]
            for r in range(count):
                reassembled[r] = total[r * rows : (r + 1) * rows].astype(bf16)
            far_row[0] = jnp.where(place[0] < 2, reassembled[count - 1], reassembled[0])
        else:
            reassembled[...] = total[...]


def finish(mine, edge, far, near, weight, half, earlier=()):
    rows, model_width = mine.shape
    channels = weight.shape[1]
    depth = model_width // FINISH_STEPS
    steps = FINISH_STEPS // 2
    wide = pl.BlockSpec((rows, depth), lambda k: (0, k + half * steps))
    block = pl.BlockSpec((rows, depth), lambda k: (0, k))
    shapes = [(rows // MAP_W, MAP_W, channels), (1, MAP_W, channels)] if half else [(rows, channels)]
    whole = lambda *x: pl.BlockSpec(x, lambda k: (0,) * len(x))
    return pl.pallas_call(
        functools.partial(finish_kernel, half),
        grid=(steps,),
        in_specs=[wide, wide, block, block]
        + [pl.BlockSpec((depth, channels), lambda k: (k + half * steps, 0))]
        + (
            [
                pl.BlockSpec(memory_space=pltpu.SMEM),
                whole(rows, channels),
                pl.BlockSpec(memory_space=pl.ANY),
            ]
            if half
            else []
        ),
        out_specs=[wide] + [whole(*x) for x in shapes],
        out_shape=[jax.ShapeDtypeStruct((rows, model_width), bf16)]
        + [jax.ShapeDtypeStruct(x, bf16 if half else f32) for x in shapes],
        scratch_shapes=[pltpu.VMEM((rows, channels), f32)],
        input_output_aliases={7: 0} if half else {},
        compiler_params=pltpu.CompilerParams(vmem_limit_bytes=VMEM_LIMIT),
        name="finish",
    )(mine, edge, far, near, weight, *earlier)


def joining_kernel_body(total_rows, pitch, place, above_far, above, middle, below, below_far, *refs):
    joining, opening, closing, out, field, feature, inner = refs[:7]
    kernels, semaphores = refs[7:10], refs[10]
    copies = [
        pltpu.make_async_copy(joining.at[a], kernels[0].at[a], semaphores.at[a]) for a in range(3)
    ]
    copies.append(pltpu.make_async_copy(opening, kernels[1], semaphores.at[3]))
    copies.append(pltpu.make_async_copy(closing, kernels[2], semaphores.at[4]))
    for copy in copies:
        copy.start()

    rows = middle.shape[0]
    field[...] = jnp.zeros_like(field)
    begin = 0
    for piece in (above_far, above, middle, below, below_far):
        for r in range(piece.shape[0]):
            field[begin : begin + MAP_W] = piece[r]
            begin += pitch

    def conv(source, kernel, waits):
        size = source.shape[0] - 2 * pitch
        sums = [None] * 3
        for a in range(3):
            for copy in waits[a]:
                copy.wait()
            window = source[a * pitch : a * pitch + size]
            for b in range(3):
                term = dot32(window, kernel[a, b])
                sums[b] = term if sums[b] is None else sums[b] + term
        return sums[1] + pltpu.roll(sums[0], 1, 0) + pltpu.roll(sums[2], size - 1, 0)

    def masked(values, margin):
        size, channels = values.shape
        shape = (size // pitch, pitch, channels)
        row = lax.broadcasted_iota(jnp.int32, shape, 0) + (place[0] * rows - margin)
        column = lax.broadcasted_iota(jnp.int32, shape, 1)
        keep = (row >= 0) & (row < total_rows) & (column < MAP_W)
        return jnp.where(keep, values.reshape(shape), 0.0).reshape(size, channels)

    waits = [[copy] for copy in copies[:3]]
    feature[...] = masked(conv(field, kernels[0], waits), 2).astype(bf16)
    rectified = jnp.maximum(feature[...], 0)
    opened = conv(rectified, kernels[1], [[copies[3]], [], []])
    inner[...] = masked(jax.nn.relu(opened), 1).astype(bf16)
    result = conv(inner, kernels[2], [[copies[4]], [], []])
    result += feature[2 * pitch : (2 + rows) * pitch].astype(f32)
    strips = [result[r * pitch : r * pitch + MAP_W] for r in range(rows)]
    out[...] = jnp.stack(strips, axis=1).astype(bf16)


def joining(reassembled, far_row, joining_weight, opening_weight, closing_weight):
    count = lax.axis_size("tensor")
    place = lax.axis_index("tensor").astype(jnp.int32)
    rows, _, channels = reassembled.shape
    features = joining_weight.shape[3]
    send = lambda value, pairs: lax.ppermute(value, "tensor", pairs)
    above = send(reassembled, [(i, i + 1) for i in range(count - 1)])
    below = send(reassembled, [(i + 1, i) for i in range(count - 1)])
    far_row = send(far_row, [(0, 2), (1, 3), (2, 0), (3, 1)])
    above_far = jnp.where(place >= 2, far_row, 0)
    below_far = jnp.where(place < 2, far_row, 0)
    pitch = round_up(MAP_W + 1, 16)
    weights = (joining_weight, opening_weight, closing_weight)
    result = pl.pallas_call(
        functools.partial(joining_kernel_body, count * rows, pitch),
        in_specs=[pl.BlockSpec(memory_space=pltpu.SMEM)]
        + [pl.BlockSpec(memory_space=pltpu.VMEM)] * 5
        + [pl.BlockSpec(memory_space=pl.ANY)] * 3,
        out_specs=pl.BlockSpec(memory_space=pltpu.VMEM),
        out_shape=jax.ShapeDtypeStruct((MAP_W, rows, features), bf16),
        scratch_shapes=[
            pltpu.VMEM(((rows + 6) * pitch, channels), bf16),
            pltpu.VMEM(((rows + 4) * pitch, features), bf16),
            pltpu.VMEM(((rows + 2) * pitch, features), bf16),
        ]
        + [pltpu.VMEM(weight.shape, bf16) for weight in weights]
        + [pltpu.SemaphoreType.DMA((5,))],
        compiler_params=pltpu.CompilerParams(vmem_limit_bytes=VMEM_LIMIT),
        name="joining",
    )(place.reshape(1), above_far, above, reassembled, below, below_far, *weights)
    return jnp.transpose(result, (1, 0, 2))


def on_device_line(
    tokens,
    query_weight,
    key_weight,
    value_weight,
    adapter_down_weight,
    query_adapter_up_weight,
    value_adapter_up_weight,
    query_norm_gain,
    key_norm_gain,
    output_weight,
    reassemble_weight,
    joining_kernel,
    opening_residual_kernel,
    closing_residual_kernel,
):
    place = lax.axis_index("tensor").astype(jnp.int32)
    images = lax.axis_size("dp")
    image = lax.axis_index("dp")
    rows, model_width = tokens.shape
    heads_width = output_weight.shape[0]
    send = lambda value, pairs: lax.ppermute(value, "tensor", pairs)
    after = lambda value, *others: lax.optimization_barrier((value, others))[0]

    rank = query_adapter_up_weight.shape[0]
    ups = (
        jnp.pad(query_adapter_up_weight, ((0, rank), (0, 0))),
        jnp.pad(value_adapter_up_weight, ((rank, 0), (0, 0))),
    )
    gains = (query_norm_gain.reshape(1, heads_width), key_norm_gain.reshape(1, heads_width))
    heads = lambda *parts, **kwargs: project(
        parts,
        (query_weight, key_weight, value_weight),
        adapter_down_weight,
        ups,
        gains,
        **kwargs,
    )

    cut = model_width // KEY_STEPS * (KEY_STEPS - LAST_STEPS)
    rest = dict(first=cut)
    inward, outward = [(0, 1), (3, 2)], [(1, 0), (2, 3)]

    (own,) = normalized_rows(tokens, (model_width,))
    up1 = send(own, [(0, 1), (1, 2), (2, 3)])
    down1 = send(own, [(1, 0), (2, 1), (3, 2)])
    (own_heads,) = heads([own])
    share = heads_width // images
    piece = lax.dynamic_slice_in_dim(output_weight, image * share, share, 0)
    piece = send(after(piece, own_heads), inward)
    share = reassemble_weight.shape[0] // images
    small = lax.dynamic_slice_in_dim(reassemble_weight, image * share, share, 0)
    small_end = send(after(small, own_heads), inward)

    up1, down1 = after((up1, down1), own_heads)
    up2 = send(up1, [(1, 2), (2, 3)])
    down2 = send(down1, [(2, 1), (1, 0)])
    up1, down1 = after((up1, down1), small_end)
    before_heads, after_heads = heads([up1], [down1])

    two = up2[:, :cut] + down2[:, :cut]
    two = [after(two, before_heads, after_heads)]
    last = [send(two[0], outward)]
    partner_weight = lax.all_gather(after(piece, two[0]), "dp", axis=0, tiled=True)
    small_two = send(after(jnp.stack([small, small_end]), two[0]), [(1, 2), (2, 1)])
    two_sums = heads([two[0]], final=False)
    up2, down2 = after((up2, down2), two_sums)
    two.append(up2[:, cut:] + down2[:, cut:])
    last.append(send(two[1], outward))
    (two_heads,) = heads([two[1]], earlier=two_sums, **rest)
    last_sums = heads([after(last[0], two_heads)], final=False)
    (last_heads,) = heads([last[1]], earlier=last_sums, **rest)
    three = jnp.stack([small, small_two[0], small_two[1]])
    three = send(after(three, last_heads), outward)

    far, near, mine, edge = attention(
        place, own_heads, before_heads, after_heads, two_heads, last_heads
    )
    far_got = send(far, inward)
    near_got = send(near, inward)
    edge_rows = edge
    edge = edge_sums(edge, output_weight)
    far_got, near_got = after((far_got, near_got), edge)
    edge = send(after(edge, far_got), outward)
    parts = []
    for half in range(2):
        if half == 1:
            far = after(far, sums)
        sums = pair_sums(far, near, far_got, near_got, output_weight, partner_weight, half)
        parts.append((send(sums[0], [(1, 3), (2, 0)]), send(sums[1], [(1, 2), (2, 1)])))
        if half == 0:
            mine_got = send(after(edge_rows, parts[0][0]), inward)
    small, small_end, small_two, three = after((small, small_end, small_two, three), far_got)
    mine = own_sums(tokens, mine, mine_got, output_weight, partner_weight)

    held = jnp.stack([small, small_end, small_two[0], small_two[1]])
    shares = jnp.where(
        place == 0,
        jnp.stack([small, three[0], three[1], three[2]]),
        jnp.where(
            place == 1,
            jnp.stack([held[1], held[0], held[2], held[3]]),
            jnp.where(
                place == 2,
                jnp.stack([held[3], held[2], held[0], held[1]]),
                jnp.stack([three[2], three[1], three[0], small]),
            ),
        ),
    )
    reassemble_full = lax.all_gather(shares, "dp", axis=1, tiled=True).reshape(
        model_width, reassemble_weight.shape[1]
    )

    layer_out, sums = finish(mine, edge, *parts[0], reassemble_full, 0)
    layer_out, reassembled, far_row = finish(
        mine, edge, *parts[1], reassemble_full, 1, (place.reshape(1), sums, layer_out)
    )
    joined_map = joining(
        reassembled, far_row, joining_kernel, opening_residual_kernel, closing_residual_kernel
    )
    return (layer_out, joined_map)


def solution(mesh):
    body = on_device_line if mesh.shape["tensor"] == 4 else on_device
    return jax.shard_map(
        body,
        mesh=mesh,
        in_specs=(
            P(("dp", "tensor"), None),
            P(None, "tensor"),
            P(None, "tensor"),
            P(None, "tensor"),
            P(),
            P(None, "tensor"),
            P(None, "tensor"),
            P("tensor"),
            P("tensor"),
            P("tensor", None),
            P("tensor", None),
            P(),
            P(),
            P(),
        ),
        out_specs=(P(("dp", "tensor"), None), P(("dp", "tensor"), None, None)),
        check_vma=False,
    )
```

```python
import functools
import math

import jax
import jax.numpy as jnp
from jax import lax
from jax.experimental import pallas as pl
from jax.experimental.pallas import tpu as pltpu
from jax.sharding import PartitionSpec as P

HEAD_DIM = 128
MAP_W = 74


epsilon = 1e-06
adapter_scale = 2.0


def padded_2(value, sides, width):
    for axis, dim in sides:
        count, length = (lax.axis_size(axis), value.shape[dim])
        up = [(i, (i + 1) % count) for i in range(count - 1)]
        down = [(j, i) for i, j in up]
        last = lax.slice_in_dim(value, length - width, length, axis=dim)
        initial = lax.slice_in_dim(value, 0, width, axis=dim)
        before = lax.ppermute(last, axis, up)
        after = lax.ppermute(initial, axis, down)
        value = jnp.concatenate([before, value, after], axis=dim)
    return value


def normalize(values):
    average = jnp.mean(values, axis=-1, keepdims=True)
    centered = values - average
    variance = jnp.mean(centered * centered, axis=-1, keepdims=True)
    return centered * lax.rsqrt(variance + epsilon)


def conv_valid(padded, kernel):
    row_count = padded.shape[0] - 2
    col_count = padded.shape[1] - 2
    running = jnp.zeros((row_count, col_count, kernel.shape[3]), jnp.float32)
    for offset_row in range(3):
        for offset_col in range(3):
            window = padded[
                offset_row : offset_row + row_count, offset_col : offset_col + col_count, :
            ]
            running = running + jnp.einsum(
                "rwc,cf->rwf",
                window,
                kernel[offset_row, offset_col],
                preferred_element_type=jnp.float32,
            )
    return running


def pad_columns(field):
    return jnp.pad(field, ((0, 0), (1, 1), (0, 0)))


def extend_rows(field):
    return padded_2(field, (("tensor", 0),), 1)


def attend(
    normalized_input,
    query_weight,
    key_weight,
    value_weight,
    adapter_down_weight,
    query_adapter_up_weight,
    value_adapter_up_weight,
    query_norm_gain,
    key_norm_gain,
):
    reduced_rows = query_adapter_up_weight.shape[0]
    reduced_output = jnp.dot(
        normalized_input, adapter_down_weight, preferred_element_type=jnp.float32
    ).astype(jnp.bfloat16)
    query_matrix = jnp.dot(
        normalized_input, query_weight, preferred_element_type=jnp.float32
    ) + adapter_scale * jnp.dot(
        reduced_output[:, :reduced_rows],
        query_adapter_up_weight,
        preferred_element_type=jnp.float32,
    )
    key_rows = jnp.dot(normalized_input, key_weight, preferred_element_type=jnp.float32)
    value_matrix = (
        jnp.dot(normalized_input, value_weight, preferred_element_type=jnp.float32)
        + adapter_scale
        * jnp.dot(
            reduced_output[:, reduced_rows:],
            value_adapter_up_weight,
            preferred_element_type=jnp.float32,
        )
    ).astype(jnp.bfloat16)
    token_count = normalized_input.shape[0]
    head_count = query_weight.shape[1] // HEAD_DIM
    shape_heads = (token_count, head_count, HEAD_DIM)
    query_heads = (
        normalize(query_matrix.reshape(shape_heads))
        * (query_norm_gain.reshape(head_count, HEAD_DIM) / math.sqrt(HEAD_DIM))
    ).astype(jnp.bfloat16)
    key_heads = (
        normalize(key_rows.reshape(shape_heads)) * key_norm_gain.reshape(head_count, HEAD_DIM)
    ).astype(jnp.bfloat16)
    scores = jnp.einsum("qhd,khd->hqk", query_heads, key_heads, preferred_element_type=jnp.float32)
    raised = jnp.exp(scores)
    softmax_weights = (raised / jnp.sum(raised, axis=-1, keepdims=True)).astype(jnp.bfloat16)
    attended = jnp.einsum(
        "hqk,khd->qhd",
        softmax_weights,
        value_matrix.reshape(shape_heads),
        preferred_element_type=jnp.float32,
    )
    return attended.astype(jnp.bfloat16).reshape(token_count, head_count * HEAD_DIM)


def on_device(
    tokens,
    query_weight,
    key_weight,
    value_weight,
    adapter_down_weight,
    query_adapter_up_weight,
    value_adapter_up_weight,
    query_norm_gain,
    key_norm_gain,
    output_weight,
    reassemble_weight,
    joining_kernel,
    opening_residual_kernel,
    closing_residual_kernel,
):
    local_rows = tokens.shape[0]
    model_width = tokens.shape[1]
    everyone = lax.all_gather(tokens, "tensor", axis=0, tiled=True)
    normalized_input = normalize(everyone.astype(jnp.float32)).astype(jnp.bfloat16)
    attended = attend(
        normalized_input,
        query_weight,
        key_weight,
        value_weight,
        adapter_down_weight,
        query_adapter_up_weight,
        value_adapter_up_weight,
        query_norm_gain,
        key_norm_gain,
    )
    partials = jnp.dot(attended, output_weight, preferred_element_type=jnp.float32)
    column_sum = lax.psum_scatter(
        partials.astype(jnp.bfloat16), "tensor", scatter_dimension=1, tiled=True
    ).astype(jnp.float32)
    slice_width = model_width // lax.axis_size("tensor")
    own_columns = lax.dynamic_slice_in_dim(
        everyone, lax.axis_index("tensor") * slice_width, slice_width, 1
    )
    layer_columns = (own_columns.astype(jnp.float32) + column_sum).astype(jnp.bfloat16)
    layer_out = lax.all_to_all(layer_columns, "tensor", split_axis=0, concat_axis=1, tiled=True)
    reassembled = lax.psum_scatter(
        jnp.dot(layer_columns, reassemble_weight, preferred_element_type=jnp.float32).astype(
            jnp.bfloat16
        ),
        "tensor",
        scatter_dimension=0,
        tiled=True,
    )
    map_strip = reassembled.reshape(local_rows // MAP_W, MAP_W, reassemble_weight.shape[1])
    rimmed = padded_2(map_strip, (("tensor", 0),), 1)
    feature = conv_valid(pad_columns(rimmed), joining_kernel).astype(jnp.bfloat16)
    inner_field = jax.nn.relu(
        conv_valid(pad_columns(extend_rows(jax.nn.relu(feature))), opening_residual_kernel)
    ).astype(jnp.bfloat16)
    joined_map = (
        conv_valid(pad_columns(extend_rows(inner_field)), closing_residual_kernel)
        + feature.astype(jnp.float32)
    ).astype(jnp.bfloat16)
    return (layer_out, joined_map)


f32 = jnp.float32
bf16 = jnp.bfloat16
KEY_STEPS = 6
FINISH_STEPS = 4
PAIR_STEPS = 4
EDGE_STEPS = 4
HEADS_STEP = 2
LAST_STEPS = 2
ROW_BLOCK = 80
VMEM_LIMIT = 56 * 1024 * 1024


def round_up(value, unit):
    return (value + unit - 1) // unit * unit


def dot32(a, b):
    return jnp.dot(a, b, preferred_element_type=f32)


def rows_kernel(tokens, *outs):
    normed = normalize(tokens[...].astype(f32)).astype(bf16)
    begin = 0
    for out in outs:
        out[...] = normed[:, begin : begin + out.shape[1]]
        begin += out.shape[1]


def normalized_rows(tokens, widths):
    rows, model_width = tokens.shape
    block = lambda width: pl.BlockSpec((ROW_BLOCK, width), lambda r: (r, 0))
    return pl.pallas_call(
        rows_kernel,
        grid=(pl.cdiv(rows, ROW_BLOCK),),
        in_specs=[block(model_width)],
        out_specs=[block(width) for width in widths],
        out_shape=[jax.ShapeDtypeStruct((rows, width), bf16) for width in widths],
        compiler_params=pltpu.CompilerParams(vmem_limit_bytes=VMEM_LIMIT),
        name="normalized_rows",
    )(tokens)


def project_kernel(count, cuts, given, final, *refs):
    pieces = len(cuts) - 1
    parts = refs[: count * pieces]
    refs = refs[count * pieces :]
    weights = refs[:3]
    down, query_up, value_up, query_gain, key_gain = refs[3:8]
    refs = refs[8:]
    earlier, refs = (refs[:2], refs[2:]) if given else (None, refs)
    outs, (totals, low) = refs[:-2], refs[-2:]
    step = pl.program_id(0)

    @pl.when(step == 0)
    def _():
        for i in range(count):
            for j in range(3):
                term = dot32(parts[i * pieces][...], weights[j][...])
                totals[i, j] = term + earlier[0][i, j] if given else term
            term = dot32(parts[i * pieces][...], down[...])
            low[i] = term + earlier[1][i] if given else term

    for p in range(pieces):

        @pl.when((step >= max(cuts[p], 1)) & (step < cuts[p + 1]))
        def _():
            for i in range(count):
                part = parts[i * pieces + p]
                for j in range(3):
                    totals[i, j] += dot32(part[...], weights[j][...])
                low[i] += dot32(part[...], down[...])

    @pl.when(step == pl.num_programs(0) - 1)
    def _():
        if not final:
            outs[0][...] = totals[...]
            outs[1][...] = low[...]
            return
        for i in range(count):
            reduced = low[i].astype(bf16)
            query = totals[i, 0] + adapter_scale * dot32(reduced, query_up[...])
            value = totals[i, 2] + adapter_scale * dot32(reduced, value_up[...])
            key = totals[i, 1]
            for h in range(query.shape[1] // HEAD_DIM):
                lanes = slice(h * HEAD_DIM, (h + 1) * HEAD_DIM)
                outs[i][0, :, lanes] = (
                    normalize(query[:, lanes]) * (query_gain[:, lanes] / math.sqrt(HEAD_DIM))
                ).astype(bf16)
                outs[i][1, :, lanes] = (
                    normalize(key[:, lanes]) * key_gain[:, lanes]
                ).astype(bf16)
            outs[i][2] = value.astype(bf16)


def project(parts, weights, down, ups, gains, first=0, earlier=(), final=True):
    count = len(parts)
    rows = parts[0][0].shape[0]
    model_width, width = weights[0].shape
    depth = model_width // KEY_STEPS
    cuts = [0]
    for piece in parts[0]:
        cuts.append(cuts[-1] + piece.shape[1] // depth)
    offset = first // depth
    rank = down.shape[1]
    whole = lambda *shape: pl.BlockSpec(shape, lambda k: (0,) * len(shape))
    piece_spec = lambda p: pl.BlockSpec(
        (rows, depth), lambda k: (0, jnp.clip(k - cuts[p], 0, cuts[p + 1] - cuts[p] - 1))
    )
    sums = [(count, 3, rows, width), (count, rows, rank)]
    results = [((3, rows, width), bf16)] * count if final else [(x, f32) for x in sums]
    result = pl.pallas_call(
        functools.partial(project_kernel, count, cuts, len(earlier) > 0, final),
        grid=(cuts[-1],),
        in_specs=[piece_spec(p) for p in range(len(cuts) - 1)] * count
        + [pl.BlockSpec((depth, width), lambda k: (k + offset, 0))] * 3
        + [pl.BlockSpec((depth, rank), lambda k: (k + offset, 0))]
        + [whole(rank, width)] * 2
        + [whole(1, width)] * 2
        + [whole(*x.shape) for x in earlier],
        out_specs=[whole(*shape) for shape, _ in results],
        out_shape=[jax.ShapeDtypeStruct(*x) for x in results],
        scratch_shapes=[pltpu.VMEM(shape, f32) for shape in sums],
        compiler_params=pltpu.CompilerParams(vmem_limit_bytes=VMEM_LIMIT),
        name="project",
    )(*(piece for block in parts for piece in block), *weights, down, *ups, *gains, *earlier)
    return result


def attention_kernel(rows, slot, place, *refs):
    blocks = refs[:5]
    outs = refs[5:9]
    query, key, value = refs[9:]
    where = place[0]

    @pl.when(pl.program_id(0) == 0)
    def _():
        for ref in (query, key, value):
            ref[...] = jnp.zeros_like(ref)
        lane = lax.broadcasted_iota(jnp.int32, (rows, HEAD_DIM), 1)
        ones = jnp.where(lane == 0, 1.0, 0.0).astype(bf16)
        for h in range(HEADS_STEP):
            for i in range(4):
                value[h, i * slot : i * slot + rows, HEAD_DIM:] = ones

    for j in range(3):
        own, before, after, two, last = (block.at[j] for block in blocks)

        def hold(i, ref):
            for h in range(HEADS_STEP):
                lanes = slice(h * HEAD_DIM, (h + 1) * HEAD_DIM)
                if j < 2:
                    (query, key)[j][h, i * slot : i * slot + rows] = ref[:, lanes]
                else:
                    value[h, i * slot : i * slot + rows, :HEAD_DIM] = ref[:, lanes]

        hold(0, own)
        hold(2, two)
        for i, end, other in ((1, 3, after), (3, 0, before)):
            pl.when(where == end)(functools.partial(hold, i, last))
            pl.when(where != end)(functools.partial(hold, i, other))

    inner = (where == 1) | (where == 2)
    far = jnp.where(inner, 2, jnp.where(where == 0, 3, 1))
    near = jnp.where(inner, jnp.where(where == 1, 1, 3), 2)
    edge = jnp.where((where == 0) | (where == 2), 1, 3)
    for asked, out in zip((far, near, 0, edge), outs):
        asked_rows = pl.ds(pl.multiple_of(asked * slot, slot), slot)
        for h in range(HEADS_STEP):
            scores = lax.dot_general(
                query[h, asked_rows],
                key[h],
                (((1,), (1,)), ((), ())),
                preferred_element_type=f32,
            )
            sums = dot32(jnp.exp(scores).astype(bf16), value[h])
            result = sums[:, :HEAD_DIM] / sums[:, HEAD_DIM : HEAD_DIM + 1]
            lanes = slice(h * HEAD_DIM, (h + 1) * HEAD_DIM)
            out[:, lanes] = result[:rows].astype(bf16)


def attention(place, *qkv):
    _, rows, width = qkv[0].shape
    slot = round_up(rows, 16)
    columns = HEADS_STEP * HEAD_DIM
    block = pl.BlockSpec((3, rows, columns), lambda h: (0, 0, h))
    return pl.pallas_call(
        functools.partial(attention_kernel, rows, slot),
        grid=(width // columns,),
        in_specs=[pl.BlockSpec(memory_space=pltpu.SMEM)] + [block] * 5,
        out_specs=[pl.BlockSpec((rows, columns), lambda h: (0, h))] * 4,
        out_shape=[jax.ShapeDtypeStruct((rows, width), bf16)] * 4,
        scratch_shapes=[
            pltpu.VMEM((HEADS_STEP, 4 * slot, HEAD_DIM), bf16),
            pltpu.VMEM((HEADS_STEP, 4 * slot, HEAD_DIM), bf16),
            pltpu.VMEM((HEADS_STEP, 4 * slot, 2 * HEAD_DIM), bf16),
        ],
        compiler_params=pltpu.CompilerParams(vmem_limit_bytes=VMEM_LIMIT),
        name="attention",
    )(place.reshape(1), *qkv)


def edge_kernel(edge, weight, out):
    out[...] = dot32(edge[...], weight[...]).astype(bf16)


def edge_sums(edge, weight):
    rows, width = edge.shape
    model_width = weight.shape[1]
    columns = model_width // EDGE_STEPS
    return pl.pallas_call(
        edge_kernel,
        grid=(EDGE_STEPS,),
        in_specs=[
            pl.BlockSpec((rows, width), lambda c: (0, 0)),
            pl.BlockSpec((width, columns), lambda c: (0, c)),
        ],
        out_specs=pl.BlockSpec((rows, columns), lambda c: (0, c)),
        out_shape=jax.ShapeDtypeStruct((rows, model_width), bf16),
        compiler_params=pltpu.CompilerParams(vmem_limit_bytes=VMEM_LIMIT),
        name="edge_sums",
    )(edge, weight)


def pair_sum_kernel(mine, other, own, got, out):
    out[...] = (dot32(mine[...], own[...]) + dot32(other[...], got[...])).astype(bf16)


def pair_sum(mine, other, own, got, half):
    rows, width = mine.shape
    model_width = own.shape[1]
    columns = model_width // PAIR_STEPS
    steps = PAIR_STEPS // 2
    operand = pl.BlockSpec((rows, width), lambda c: (0, 0))
    weight = pl.BlockSpec((width, columns), lambda c: (0, c + half * steps))
    return pl.pallas_call(
        pair_sum_kernel,
        grid=(steps,),
        in_specs=[operand] * 2 + [weight] * 2,
        out_specs=pl.BlockSpec((rows, columns), lambda c: (0, c)),
        out_shape=jax.ShapeDtypeStruct((rows, model_width // 2), bf16),
        compiler_params=pltpu.CompilerParams(vmem_limit_bytes=VMEM_LIMIT),
        name="pair_sum",
    )(mine, other, own, got)


def own_kernel(tokens, mine, other, own, got, out):
    out[...] = tokens[...].astype(f32) + (
        dot32(mine[...], own[...]) + dot32(other[...], got[...])
    )


def own_sums(tokens, mine, other, own, got):
    rows, width = mine.shape
    model_width = own.shape[1]
    columns = model_width // PAIR_STEPS
    operand = pl.BlockSpec((rows, width), lambda c: (0, 0))
    weight = pl.BlockSpec((width, columns), lambda c: (0, c))
    block = pl.BlockSpec((rows, columns), lambda c: (0, c))
    return pl.pallas_call(
        own_kernel,
        grid=(PAIR_STEPS,),
        in_specs=[block, operand, operand, weight, weight],
        out_specs=block,
        out_shape=jax.ShapeDtypeStruct((rows, model_width), f32),
        compiler_params=pltpu.CompilerParams(vmem_limit_bytes=VMEM_LIMIT),
        name="own_sums",
    )(tokens, mine, other, own, got)


def finish_kernel(half, mine, edge, far, near, weight, *refs):
    if half:
        place, earlier, _, layer_out, reassembled, far_row, total = refs
    else:
        layer_out, reassembled, total = refs
    step = pl.program_id(0)
    layer = (
        mine[...] + edge[...].astype(f32) + far[...].astype(f32) + near[...].astype(f32)
    ).astype(bf16)
    layer_out[...] = layer
    term = dot32(layer, weight[...])

    @pl.when(step == 0)
    def _():
        total[...] = term + earlier[...] if half else term

    @pl.when(step > 0)
    def _():
        total[...] += term

    @pl.when(step == pl.num_programs(0) - 1)
    def _():
        if half:
            rows = reassembled.shape[1]
            count = reassembled.shape[0]
            for r in range(count):
                reassembled[r] = total[r * rows : (r + 1) * rows].astype(bf16)
            far_row[0] = jnp.where(place[0] < 2, reassembled[count - 1], reassembled[0])
        else:
            reassembled[...] = total[...]


def finish(mine, edge, far, near, weight, half, earlier=()):
    rows, model_width = mine.shape
    channels = weight.shape[1]
    depth = model_width // FINISH_STEPS
    steps = FINISH_STEPS // 2
    wide = pl.BlockSpec((rows, depth), lambda k: (0, k + half * steps))
    block = pl.BlockSpec((rows, depth), lambda k: (0, k))
    shapes = [(rows // MAP_W, MAP_W, channels), (1, MAP_W, channels)] if half else [(rows, channels)]
    whole = lambda *x: pl.BlockSpec(x, lambda k: (0,) * len(x))
    return pl.pallas_call(
        functools.partial(finish_kernel, half),
        grid=(steps,),
        in_specs=[wide, wide, block, block]
        + [pl.BlockSpec((depth, channels), lambda k: (k + half * steps, 0))]
        + (
            [
                pl.BlockSpec(memory_space=pltpu.SMEM),
                whole(rows, channels),
                pl.BlockSpec(memory_space=pl.ANY),
            ]
            if half
            else []
        ),
        out_specs=[wide] + [whole(*x) for x in shapes],
        out_shape=[jax.ShapeDtypeStruct((rows, model_width), bf16)]
        + [jax.ShapeDtypeStruct(x, bf16 if half else f32) for x in shapes],
        scratch_shapes=[pltpu.VMEM((rows, channels), f32)],
        input_output_aliases={7: 0} if half else {},
        compiler_params=pltpu.CompilerParams(vmem_limit_bytes=VMEM_LIMIT),
        name="finish",
    )(mine, edge, far, near, weight, *earlier)


def joining_kernel_body(total_rows, pitch, place, above_far, above, middle, below, below_far, *refs):
    joining, opening, closing, out, field, feature, inner = refs[:7]
    kernels, semaphores = refs[7:10], refs[10]
    copies = [
        pltpu.make_async_copy(joining.at[a], kernels[0].at[a], semaphores.at[a]) for a in range(3)
    ]
    copies.append(pltpu.make_async_copy(opening, kernels[1], semaphores.at[3]))
    copies.append(pltpu.make_async_copy(closing, kernels[2], semaphores.at[4]))
    for copy in copies:
        copy.start()

    rows = middle.shape[0]
    field[...] = jnp.zeros_like(field)
    begin = 0
    for piece in (above_far, above, middle, below, below_far):
        for r in range(piece.shape[0]):
            field[begin : begin + MAP_W] = piece[r]
            begin += pitch

    def conv(source, kernel, waits):
        size = source.shape[0] - 2 * pitch
        sums = [None] * 3
        for a in range(3):
            for copy in waits[a]:
                copy.wait()
            window = source[a * pitch : a * pitch + size]
            for b in range(3):
                term = dot32(window, kernel[a, b])
                sums[b] = term if sums[b] is None else sums[b] + term
        return sums[1] + pltpu.roll(sums[0], 1, 0) + pltpu.roll(sums[2], size - 1, 0)

    def masked(values, margin):
        size, channels = values.shape
        shape = (size // pitch, pitch, channels)
        row = lax.broadcasted_iota(jnp.int32, shape, 0) + (place[0] * rows - margin)
        column = lax.broadcasted_iota(jnp.int32, shape, 1)
        keep = (row >= 0) & (row < total_rows) & (column < MAP_W)
        return jnp.where(keep, values.reshape(shape), 0.0).reshape(size, channels)

    waits = [[copy] for copy in copies[:3]]
    feature[...] = masked(conv(field, kernels[0], waits), 2).astype(bf16)
    rectified = jnp.maximum(feature[...], 0)
    opened = conv(rectified, kernels[1], [[copies[3]], [], []])
    inner[...] = masked(jax.nn.relu(opened), 1).astype(bf16)
    result = conv(inner, kernels[2], [[copies[4]], [], []])
    result += feature[2 * pitch : (2 + rows) * pitch].astype(f32)
    strips = [result[r * pitch : r * pitch + MAP_W] for r in range(rows)]
    out[...] = jnp.stack(strips, axis=1).astype(bf16)


def joining(reassembled, far_row, joining_weight, opening_weight, closing_weight):
    count = lax.axis_size("tensor")
    place = lax.axis_index("tensor").astype(jnp.int32)
    rows, _, channels = reassembled.shape
    features = joining_weight.shape[3]
    send = lambda value, pairs: lax.ppermute(value, "tensor", pairs)
    above = send(reassembled, [(i, i + 1) for i in range(count - 1)])
    below = send(reassembled, [(i + 1, i) for i in range(count - 1)])
    far_row = send(far_row, [(0, 2), (1, 3), (2, 0), (3, 1)])
    above_far = jnp.where(place >= 2, far_row, 0)
    below_far = jnp.where(place < 2, far_row, 0)
    pitch = round_up(MAP_W + 1, 16)
    weights = (joining_weight, opening_weight, closing_weight)
    result = pl.pallas_call(
        functools.partial(joining_kernel_body, count * rows, pitch),
        in_specs=[pl.BlockSpec(memory_space=pltpu.SMEM)]
        + [pl.BlockSpec(memory_space=pltpu.VMEM)] * 5
        + [pl.BlockSpec(memory_space=pl.ANY)] * 3,
        out_specs=pl.BlockSpec(memory_space=pltpu.VMEM),
        out_shape=jax.ShapeDtypeStruct((MAP_W, rows, features), bf16),
        scratch_shapes=[
            pltpu.VMEM(((rows + 6) * pitch, channels), bf16),
            pltpu.VMEM(((rows + 4) * pitch, features), bf16),
            pltpu.VMEM(((rows + 2) * pitch, features), bf16),
        ]
        + [pltpu.VMEM(weight.shape, bf16) for weight in weights]
        + [pltpu.SemaphoreType.DMA((5,))],
        compiler_params=pltpu.CompilerParams(vmem_limit_bytes=VMEM_LIMIT),
        name="joining",
    )(place.reshape(1), above_far, above, reassembled, below, below_far, *weights)
    return jnp.transpose(result, (1, 0, 2))


def on_device_line(
    tokens,
    query_weight,
    key_weight,
    value_weight,
    adapter_down_weight,
    query_adapter_up_weight,
    value_adapter_up_weight,
    query_norm_gain,
    key_norm_gain,
    output_weight,
    reassemble_weight,
    joining_kernel,
    opening_residual_kernel,
    closing_residual_kernel,
):
    place = lax.axis_index("tensor").astype(jnp.int32)
    images = lax.axis_size("dp")
    image = lax.axis_index("dp")
    rows, model_width = tokens.shape
    heads_width = output_weight.shape[0]
    send = lambda value, pairs: lax.ppermute(value, "tensor", pairs)
    after = lambda value, *others: lax.optimization_barrier((value, others))[0]

    rank = query_adapter_up_weight.shape[0]
    ups = (
        jnp.pad(query_adapter_up_weight, ((0, rank), (0, 0))),
        jnp.pad(value_adapter_up_weight, ((rank, 0), (0, 0))),
    )
    gains = (query_norm_gain.reshape(1, heads_width), key_norm_gain.reshape(1, heads_width))
    heads = lambda *parts, **kwargs: project(
        parts,
        (query_weight, key_weight, value_weight),
        adapter_down_weight,
        ups,
        gains,
        **kwargs,
    )

    cut = model_width // KEY_STEPS * (KEY_STEPS - LAST_STEPS)
    rest = dict(first=cut)
    inward, outward = [(0, 1), (3, 2)], [(1, 0), (2, 3)]

    (own,) = normalized_rows(tokens, (model_width,))
    up1 = send(own, [(0, 1), (1, 2), (2, 3)])
    down1 = send(own, [(1, 0), (2, 1), (3, 2)])
    (own_heads,) = heads([own])
    share = heads_width // images
    piece = lax.dynamic_slice_in_dim(output_weight, image * share, share, 0)
    piece = send(after(piece, own_heads), inward)
    share = reassemble_weight.shape[0] // images
    small = lax.dynamic_slice_in_dim(reassemble_weight, image * share, share, 0)
    small_end = send(after(small, own_heads), inward)

    up1, down1 = after((up1, down1), own_heads)
    up2 = send(up1, [(1, 2), (2, 3)])
    down2 = send(down1, [(2, 1), (1, 0)])
    up1, down1 = after((up1, down1), small_end)
    before_heads, after_heads = heads([up1], [down1])

    two = up2[:, :cut] + down2[:, :cut]
    two = [after(two, before_heads, after_heads)]
    last = [send(two[0], outward)]
    partner_weight = lax.all_gather(after(piece, two[0]), "dp", axis=0, tiled=True)
    small_two = send(after(jnp.stack([small, small_end]), two[0]), [(1, 2), (2, 1)])
    two_sums = heads([two[0]], final=False)
    up2, down2 = after((up2, down2), two_sums)
    two.append(up2[:, cut:] + down2[:, cut:])
    last.append(send(two[1], outward))
    (two_heads,) = heads([two[1]], earlier=two_sums, **rest)
    last_sums = heads([after(last[0], two_heads)], final=False)
    (last_heads,) = heads([last[1]], earlier=last_sums, **rest)
    three = jnp.stack([small, small_two[0], small_two[1]])
    three = send(after(three, last_heads), outward)

    far, near, mine, edge = attention(
        place, own_heads, before_heads, after_heads, two_heads, last_heads
    )
    far_got = send(far, inward)
    near_got = send(near, inward)
    edge_rows = edge
    edge = edge_sums(edge, output_weight)
    far_got, near_got = after((far_got, near_got), edge)
    edge = send(after(edge, far_got), outward)
    parts = []
    for half in range(2):
        if half == 1:
            far = after(far, near_sum)
        far_sum = pair_sum(far, far_got, output_weight, partner_weight, half)
        near = after(near, far_sum)
        near_sum = pair_sum(near, near_got, output_weight, partner_weight, half)
        parts.append((send(far_sum, [(1, 3), (2, 0)]), send(near_sum, [(1, 2), (2, 1)])))
        if half == 0:
            mine_got = send(after(edge_rows, parts[0][0]), inward)
    small, small_end, small_two, three = after((small, small_end, small_two, three), far_got)
    mine = own_sums(tokens, mine, mine_got, output_weight, partner_weight)

    held = jnp.stack([small, small_end, small_two[0], small_two[1]])
    shares = jnp.where(
        place == 0,
        jnp.stack([small, three[0], three[1], three[2]]),
        jnp.where(
            place == 1,
            jnp.stack([held[1], held[0], held[2], held[3]]),
            jnp.where(
                place == 2,
                jnp.stack([held[3], held[2], held[0], held[1]]),
                jnp.stack([three[2], three[1], three[0], small]),
            ),
        ),
    )
    reassemble_full = lax.all_gather(shares, "dp", axis=1, tiled=True).reshape(
        model_width, reassemble_weight.shape[1]
    )

    layer_out, sums = finish(mine, edge, *parts[0], reassemble_full, 0)
    layer_out, reassembled, far_row = finish(
        mine, edge, *parts[1], reassemble_full, 1, (place.reshape(1), sums, layer_out)
    )
    joined_map = joining(
        reassembled, far_row, joining_kernel, opening_residual_kernel, closing_residual_kernel
    )
    return (layer_out, joined_map)


def solution(mesh):
    body = on_device_line if mesh.shape["tensor"] == 4 else on_device
    return jax.shard_map(
        body,
        mesh=mesh,
        in_specs=(
            P(("dp", "tensor"), None),
            P(None, "tensor"),
            P(None, "tensor"),
            P(None, "tensor"),
            P(),
            P(None, "tensor"),
            P(None, "tensor"),
            P("tensor"),
            P("tensor"),
            P("tensor", None),
            P("tensor", None),
            P(),
            P(),
            P(),
        ),
        out_specs=(P(("dp", "tensor"), None), P(("dp", "tensor"), None, None)),
        check_vma=False,
    )
```
